512 devices in a mesh: seq: 32 (over y, x, core), head: 16 (over z).
Axes of the slice: x: 4, y: 4, z: 16, core: 2. Of those that a mesh axis runs over, the one named last changes fastest.
Arguments:
- queries: bfloat16 [256, 128, 192], P('seq', 'head'), may hold values from -260 to 260
- prompt_cache: bfloat16 [32768, 576], P('seq'), may hold values from -8 to 8
- suffix_cache: bfloat16 [64, 256, 576], P('seq'), may hold values from -6 to 6
- gen_lengths: int32 [64], P('seq'), may hold values from 1 to 256
- new_latent: bfloat16 [256, 512], P('seq', 'head'), may hold values from -24 to 24
- new_rope: bfloat16 [256, 64], P('seq'), may hold values from -6 to 6
- latent_gain: bfloat16 [512], P('head'), may hold values from 0.25 to 1.75
- w_uk: bfloat16 [128, 128, 512], P('head'), may hold values from -0.5 to 0.5
- w_uv: bfloat16 [128, 512, 128], P('head'), may hold values from -0.25 to 0.25
Outputs:
- attn_values: bfloat16 [256, 16384], P('seq', 'head')
The draws below stay inside these ranges and needn't reach their ends.
All inputs are finite; a program needn't handle non-finite values.
Results may differ from the reference program's by a relative error of at most 0.0075.
Values may be sent and summed in bfloat16 or wider, within the bound.
No kernel may reach another device: no remote copies, remote signals or barrier semaphores. Data moves between devices by JAX's collectives and lax.ppermute only.
A program may use at most 64 MiB of HBM per device.

```python
import jax
import jax.numpy as jnp
from jax import lax

HEADS = 128
NOPE = 128
ROPE = 64
LATENT = 512
VALUE = 128
SAMPLES = 64
STEPS = 4
GEN = 256
PROMPT = 32768
QROWS = 256


def shared_cache(key):
    return jnp.clip(jax.random.normal(key, (PROMPT, LATENT + ROPE), jnp.float32), -5.0, 5.0)


def shared_rope(key):
    inner = jax.random.fold_in(key, 101)
    return 1.5 * jnp.clip(jax.random.normal(inner, (QROWS, ROPE), jnp.float32), -4.0, 4.0)


def draw_prompt_cache(key, part):
    values = shared_cache(key)
    return values.astype(jnp.bfloat16)


def draw_queries(key, part):
    common = shared_rope(key)
    key = jax.random.fold_in(key, 12)
    values = jnp.clip(jax.random.normal(key, (QROWS, HEADS, NOPE + ROPE), jnp.float32), -6.0, 6.0)
    values = jnp.concatenate([values[:, :, :NOPE], values[:, :, NOPE:] + common[:, None, :]], -1)
    return values.astype(jnp.bfloat16)


def draw_new_rope(key, part):
    values = shared_rope(key)
    return values.astype(jnp.bfloat16)


def draw_new_latent(key, part):
    key = jax.random.fold_in(key, 14)
    ramp = jnp.arange(LATENT).astype(jnp.float32) / float(LATENT - 1)
    values = jnp.clip(jax.random.normal(key, (QROWS, LATENT), jnp.float32), -6.0, 6.0)
    values = values * (1.0 + 3.0 * ramp)[None, :]
    return values.astype(jnp.bfloat16)


def draw_gen_lengths(key, part):
    key = jax.random.fold_in(key, 13)
    first, second = jax.random.split(key)
    counts = jax.random.randint(first, (SAMPLES,), 1, GEN + 1)
    picked = jax.random.randint(second, (), 0, SAMPLES)
    return jnp.where(jnp.arange(SAMPLES) == picked, GEN, counts).astype(jnp.int32)


def block_levels(rng, extent, pieces, low, largest):
    level, own = 1.0, jax.random.fold_in(rng, 6)
    for axis_at, parts in pieces:
        draws = jnp.exp(jax.random.uniform(jax.random.fold_in(own, axis_at), (parts,), jnp.float32, low / len(pieces), largest / len(pieces)))
        level = level * jnp.repeat(draws, extent[axis_at] // parts).reshape([-1 if axis == axis_at else 1 for axis in range(len(extent))])
    return level


def normal_values(rng, dims, scale, limit, shards=(), kind=jnp.bfloat16):
    factor_of = block_levels(rng, dims, shards, -0.22, 0.18) if shards else 1.0
    array = jax.random.normal(rng, dims, jnp.float32) * scale * factor_of
    return jnp.minimum(jnp.maximum(array, -limit), limit).astype(kind)


def setup_inputs(seed: int = 0) -> dict:
    splits = jax.random.split(jax.random.key(seed), 10)
    return {
        "queries": draw_queries(jax.random.fold_in(splits[9], 71), 0),
        "prompt_cache": draw_prompt_cache(jax.random.fold_in(splits[9], 71), 0),
        "suffix_cache": normal_values(splits[2], (SAMPLES, GEN, LATENT + ROPE), 1.0, 6.0, ((0, 32),)),
        "gen_lengths": draw_gen_lengths(jax.random.fold_in(splits[9], 71), 0),
        "new_latent": draw_new_latent(jax.random.fold_in(splits[9], 71), 0),
        "new_rope": draw_new_rope(jax.random.fold_in(splits[9], 71), 0),
        "latent_gain": jnp.clip(1.0 + 0.15 * jax.random.normal(splits[6], (LATENT,), jnp.float32), 0.25, 1.75).astype(jnp.bfloat16),
        "w_uk": normal_values(splits[7], (HEADS, NOPE, LATENT), NOPE ** -0.5, 0.5, ((0, 16),)),
        "w_uv": normal_values(splits[8], (HEADS, LATENT, VALUE), LATENT ** -0.5, 0.25, ((0, 16),)),
    }


eps = 1e-06

def reference(queries, prompt_cache, suffix_cache, gen_lengths, new_latent, new_rope, latent_gain, w_uk, w_uv):
    plain = new_latent.astype(jnp.float32)
    normed = (plain * lax.rsqrt(lax.optimization_barrier(jnp.mean(plain * plain, -1, keepdims=True)) + eps) * latent_gain.astype(jnp.float32)).astype(jnp.bfloat16)
    new_keys = jnp.concatenate([normed, new_rope], -1).reshape(SAMPLES, STEPS, LATENT + ROPE)
    scale = float(NOPE + ROPE) ** (-0.5)
    live = jnp.arange(GEN)[None, None, :] < gen_lengths[:, None, None]
    causal = (jnp.arange(STEPS)[None, :] <= jnp.arange(STEPS)[:, None])[None, :, :]
    suffix_f = suffix_cache.astype(jnp.float32)
    new_f = new_keys.astype(jnp.float32)

    def one_head(operands):
        query_head, key_map, value_map = operands
        absorbed = jnp.dot(query_head[:, :NOPE], key_map, preferred_element_type=jnp.float32).astype(jnp.bfloat16)
        full = jnp.concatenate([absorbed, query_head[:, NOPE:]], -1)
        full_f = full.astype(jnp.float32)
        prompt_scores = jnp.dot(full, prompt_cache.T, preferred_element_type=jnp.float32) * scale
        grouped = full_f.reshape(SAMPLES, STEPS, LATENT + ROPE)
        suffix_scores = jnp.einsum('btc,bgc->btg', grouped, suffix_f) * scale
        suffix_scores = jnp.where(live, suffix_scores, -jnp.inf)
        fresh_scores = jnp.einsum('btc,buc->btu', grouped, new_f) * scale
        fresh_scores = jnp.where(causal, fresh_scores, -jnp.inf)
        peak = jnp.maximum(lax.optimization_barrier(jnp.max(prompt_scores, -1)).reshape(SAMPLES, STEPS), jnp.maximum(lax.optimization_barrier(jnp.max(suffix_scores, -1)), lax.optimization_barrier(jnp.max(fresh_scores, -1))))
        prompt_exp = jnp.exp(prompt_scores - peak.reshape(QROWS)[:, None])
        suffix_exp = jnp.exp(suffix_scores - peak[:, :, None])
        fresh_exp = jnp.exp(fresh_scores - peak[:, :, None])
        total = lax.optimization_barrier(jnp.sum(prompt_exp, -1)).reshape(SAMPLES, STEPS) + lax.optimization_barrier(jnp.sum(suffix_exp, -1)) + lax.optimization_barrier(jnp.sum(fresh_exp, -1))
        summed = jnp.dot(prompt_exp.astype(jnp.bfloat16), prompt_cache[:, :LATENT], preferred_element_type=jnp.float32).reshape(SAMPLES, STEPS, LATENT)
        summed = summed + jnp.einsum('btg,bgl->btl', suffix_exp.astype(jnp.bfloat16).astype(jnp.float32), suffix_f[:, :, :LATENT])
        summed = summed + jnp.einsum('btu,bul->btl', fresh_exp.astype(jnp.bfloat16).astype(jnp.float32), new_f[:, :, :LATENT])
        attn_latent = (summed / total[:, :, None]).astype(jnp.bfloat16).reshape(QROWS, LATENT)
        return jnp.dot(attn_latent, value_map, preferred_element_type=jnp.float32).astype(jnp.bfloat16)
    per_head = lax.map(one_head, (jnp.transpose(queries, (1, 0, 2)), w_uk, w_uv))
    return jnp.transpose(per_head, (1, 0, 2)).reshape(QROWS, HEADS * VALUE)
```

```python
import functools

import jax
import jax.numpy as jnp
from jax import lax
from jax.experimental import pallas as pl
from jax.experimental.pallas import tpu as pltpu
from jax.sharding import Mesh
from jax.sharding import PartitionSpec as P

eps = 1e-06
LOG2E = 1.4426950408889634
CHIPS = 16
PLANE = ("y", "x")
F32 = jnp.float32
BF16 = jnp.bfloat16
VMEM = pltpu.VMEM
NT = (((1,), (1,)), ((), ()))


def split3(value):
    high = value.astype(BF16).astype(F32)
    rest = value - high
    middle = rest.astype(BF16).astype(F32)
    return high, middle, (rest - middle).astype(BF16).astype(F32)


def pre_kernel(queries_ref, sent_ref):
    by_head = jnp.swapaxes(queries_ref[...].astype(F32), 0, 1)
    rows = by_head.reshape(64, by_head.shape[2]).astype(BF16)
    for chip in range(CHIPS):
        sent_ref[chip] = rows


def main_kernel(scale, q_ref, ka_ref, kb_ref, wuk_ref, wuv_ref, out_ref):
    latent = wuk_ref.shape[2]
    nope = wuk_ref.shape[1]
    lane = lax.broadcasted_iota(jnp.int32, (128, 128), 1)
    stats = jnp.zeros((128, 128), F32)
    for pair in range(4):
        both = q_ref[:, 16 * pair : 16 * pair + 16, :].astype(F32).reshape(CHIPS, 2, 8, -1)
        fulls = []
        for j in range(2):
            one = both[:, j].reshape(128, -1).astype(BF16)
            absorbed = jnp.dot(
                one[:, :nope], wuk_ref[2 * pair + j], preferred_element_type=F32
            ).astype(BF16)
            fulls.append(jnp.concatenate([absorbed, one[:, nope:]], -1))
        full = jnp.concatenate(fulls, 0)
        sa = lax.dot_general(full, ka_ref[...], NT, preferred_element_type=F32)
        sb = lax.dot_general(full, kb_ref[...], NT, preferred_element_type=F32)
        peak = jnp.maximum(jnp.max(sa, -1, keepdims=True), jnp.max(sb, -1, keepdims=True))
        pa = jnp.exp2((sa - peak) * (scale * LOG2E))
        pb = jnp.exp2((sb - peak) * (scale * LOG2E))
        mass = jnp.sum(pa, -1, keepdims=True) + jnp.sum(pb, -1, keepdims=True)
        acc = jnp.dot(pa.astype(BF16), ka_ref[:, :latent], preferred_element_type=F32)
        acc = acc + jnp.dot(pb.astype(BF16), kb_ref[:, :latent], preferred_element_type=F32)
        attn = (acc / mass).astype(BF16)
        values = []
        for j in range(2):
            head = 2 * pair + j
            here = slice(128 * j, 128 * j + 128)
            values.append(
                jnp.dot(attn[here], wuv_ref[head], preferred_element_type=F32).reshape(
                    CHIPS, 8, 128
                )
            )
            for k, piece in enumerate(split3(peak[here]) + split3(mass[here])):
                stats = jnp.where(lane == 8 * k + head, piece, stats)
        out_ref[:, 16 * pair : 16 * pair + 16, :] = jnp.concatenate(values, 1).astype(BF16)
    stats = stats.reshape(CHIPS, 8, 128)
    out_ref[:, 64:80, :] = jnp.concatenate([stats, jnp.zeros_like(stats)], 1).astype(BF16)


def local_kernel(
    scale, q_ref, suffix_ref, lengths_ref, rope_ref, new_ref, wuk_ref, wuv_ref, out_ref, stats_ref
):
    nope, latent = wuk_ref.shape[1:]
    q = q_ref[0]
    width = q.shape[1]
    q32 = q.astype(F32)
    parts = []
    for pair in range(4):
        two = q[16 * pair : 16 * pair + 16, :nope]
        first = jnp.dot(two, wuk_ref[2 * pair], preferred_element_type=F32)
        second = jnp.dot(two, wuk_ref[2 * pair + 1], preferred_element_type=F32)
        parts += [first[:8], second[8:]]
    absorbed = jnp.concatenate(parts, 0)
    full = jnp.concatenate([absorbed, q32[:, nope:]], -1).astype(BF16)

    pieces = new_ref[...].astype(F32)
    new = jnp.concatenate(
        [
            pieces[4 * g] + pieces[4 * g + 1] + pieces[4 * g + 2] + pieces[4 * g + 3]
            for g in range(4)
        ],
        -1,
    )
    plain, gain = new[:8], new[8:9]
    square = jnp.sum(plain * plain, -1, keepdims=True) / latent
    normed = plain * lax.rsqrt(square + eps) * gain
    fresh = jnp.concatenate([normed, rope_ref[...].astype(F32)], -1)
    fresh = jnp.concatenate([fresh, jnp.zeros((120, fresh.shape[1]), F32)], 0).astype(BF16)

    gen = suffix_ref.shape[1]
    row = lax.broadcasted_iota(jnp.int32, (64, gen), 0) % 8
    col = lax.broadcasted_iota(jnp.int32, (64, gen), 1)
    scores, keys = [], []
    for sample in range(2):
        block = suffix_ref[sample]
        raw = lax.dot_general(full, block, NT, preferred_element_type=F32)
        live = (row // 4 == sample) & (col < lengths_ref[sample])
        scores.append(jnp.where(live, raw, -jnp.inf))
        keys.append(block[:, :latent])
    raw = lax.dot_general(full, fresh, NT, preferred_element_type=F32)
    row, col = row[:, :128], col[:, :128]
    live = (col < 8) & (col // 4 == row // 4) & (col <= row)
    scores.append(jnp.where(live, raw, -jnp.inf))
    keys.append(fresh[:, :latent])
    peak = functools.reduce(jnp.maximum, [jnp.max(s, -1, keepdims=True) for s in scores])
    mass, acc = 0.0, 0.0
    for s, v in zip(scores, keys):
        p = jnp.exp2((s - peak) * (scale * LOG2E))
        mass = mass + jnp.sum(p, -1, keepdims=True)
        acc = acc + jnp.dot(p.astype(BF16), v, preferred_element_type=F32)
    attn = (acc / mass).astype(BF16)
    lane = lax.broadcasted_iota(jnp.int32, (8, 128), 1)
    stats = jnp.zeros((8, 128), F32)
    for pair in range(4):
        two = attn[16 * pair : 16 * pair + 16]
        first = jnp.dot(two, wuv_ref[2 * pair], preferred_element_type=F32)
        second = jnp.dot(two, wuv_ref[2 * pair + 1], preferred_element_type=F32)
        out_ref[16 * pair : 16 * pair + 8, :] = first[:8]
        out_ref[16 * pair + 8 : 16 * pair + 16, :] = second[8:]
    for head in range(8):
        here = slice(8 * head, 8 * head + 8)
        stats = jnp.where(lane == head, peak[here], stats)
        stats = jnp.where(lane == 8 + head, mass[here], stats)
    stats_ref[...] = stats


def combine_kernel(scale, got_ref, own_ref, own_stats_ref, out_ref):
    raw = got_ref[:, 64:80, :].astype(F32)[:, :8, :].reshape(128, 128)

    def lanes(k):
        return raw if k == 0 else pltpu.roll(raw, 128 - 8 * k, 1)

    peaks = (lanes(0) + lanes(1) + lanes(2)).reshape(CHIPS, 8, 128)
    masses = (lanes(3) + lanes(4) + lanes(5)).reshape(CHIPS, 8, 128)
    own_peak = own_stats_ref[...]
    own_mass = pltpu.roll(own_peak, 128 - 8, 1)
    peak = jnp.maximum(jnp.max(peaks, 0), own_peak)
    weights = jnp.exp2((peaks - peak[None]) * (scale * LOG2E)) * masses
    own_weight = jnp.exp2((own_peak - peak) * (scale * LOG2E)) * own_mass
    inverse = 1.0 / (jnp.sum(weights, 0) + own_weight)
    for pair in range(4):
        got = got_ref[:, 16 * pair : 16 * pair + 16, :].astype(F32)
        for j in range(2):
            head = 2 * pair + j
            total = own_weight[:, head : head + 1] * own_ref[8 * head : 8 * head + 8, :]
            for chip in range(CHIPS):
                total = total + weights[chip, :, head : head + 1] * got[chip, 8 * j : 8 * j + 8, :]
            total = total * inverse[:, head : head + 1]
            out_ref[:, 128 * head : 128 * head + 128] = total.astype(BF16)


def call(kernel, outs, n_in, smem=()):
    return pl.pallas_call(
        kernel,
        out_shape=outs,
        in_specs=[
            pl.BlockSpec(memory_space=pltpu.SMEM if i in smem else VMEM) for i in range(n_in)
        ],
        out_specs=jax.tree.map(lambda _: pl.BlockSpec(memory_space=VMEM), outs),
        compiler_params=pltpu.CompilerParams(vmem_limit_bytes=48 * 1024 * 1024),
    )


def per_device(
    queries, prompt_cache, suffix_cache, gen_lengths, new_latent, new_rope, latent_gain, w_uk, w_uv
):
    width = queries.shape[2]
    scale = float(width) ** (-0.5)
    other = lax.ppermute(prompt_cache, "core", [(0, 1), (1, 0)])
    sent = call(pre_kernel, jax.ShapeDtypeStruct((CHIPS, 64, width), BF16), 1)(queries)
    gathered = lax.all_to_all(sent, PLANE, 0, 0, tiled=True)

    place = lax.axis_index("z") % 4
    mine = jnp.concatenate([new_latent, latent_gain[None]], 0)
    mine = jnp.tile(jnp.pad(mine, ((0, 7), (0, 0))), (1, 4))
    mine = jnp.where(jnp.arange(128)[None] // 32 == place, mine, 0)
    news = lax.all_to_all(jnp.broadcast_to(mine[None], (16, 16, 128)), "z", 0, 0, tiled=True)

    parts = call(
        functools.partial(main_kernel, scale), jax.ShapeDtypeStruct((CHIPS, 80, 128), BF16), 5
    )(gathered, prompt_cache, other, w_uk, w_uv)
    got = lax.all_to_all(parts, PLANE, 0, 0, tiled=True)
    own, own_stats = call(
        functools.partial(local_kernel, scale),
        (jax.ShapeDtypeStruct((64, 128), F32), jax.ShapeDtypeStruct((8, 128), F32)),
        7,
        smem=(2,),
    )(sent, suffix_cache, gen_lengths, new_rope, news, w_uk, w_uv)
    return call(
        functools.partial(combine_kernel, scale), jax.ShapeDtypeStruct((8, 1024), BF16), 3
    )(got, own, own_stats)


def solution(mesh):
    fine = Mesh(mesh.devices.reshape(4, 4, 2, 16), ("y", "x", "core", "z"))
    seq = ("y", "x", "core")
    return jax.shard_map(
        per_device,
        mesh=fine,
        in_specs=(
            P(seq, "z", None),
            P(seq, None),
            P(seq, None, None),
            P(seq),
            P(seq, "z"),
            P(seq, None),
            P("z"),
            P("z", None, None),
            P("z", None, None),
        ),
        out_specs=P(seq, "z"),
        check_vma=False,
    )
```

```python
import functools

import jax
import jax.numpy as jnp
from jax import lax
from jax.experimental import pallas as pl
from jax.experimental.pallas import tpu as pltpu
from jax.sharding import Mesh
from jax.sharding import PartitionSpec as P

eps = 1e-06
LOG2E = 1.4426950408889634
CHIPS = 16
PLANE = ("y", "x")
F32 = jnp.float32
BF16 = jnp.bfloat16
VMEM = pltpu.VMEM
NT = (((1,), (1,)), ((), ()))


def split3(value):
    high = value.astype(BF16).astype(F32)
    rest = value - high
    middle = rest.astype(BF16).astype(F32)
    return high, middle, (rest - middle).astype(BF16).astype(F32)


def queries_kernel(queries_ref, sent_ref):
    by_head = jnp.swapaxes(queries_ref[...].astype(F32), 0, 1)
    rows = by_head.reshape(64, by_head.shape[2]).astype(BF16)
    for chip in range(CHIPS):
        sent_ref[chip] = rows


def own_kernel(q_ref, latent_ref, gain_ref, wuk_ref, mine_ref, full_ref):
    latents = latent_ref[...].astype(F32)
    gain = jnp.concatenate([gain_ref[...].astype(F32), jnp.zeros((3, 32), F32)], 0)
    mine = [latents[:4], latents[4:], gain, jnp.zeros((4, 32), F32)]
    mine = jnp.concatenate(mine, 1).astype(BF16)
    for device in range(16):
        mine_ref[device] = mine
    nope = wuk_ref.shape[1]
    q = q_ref[0]
    parts = []
    for pair in range(4):
        two = q[16 * pair : 16 * pair + 16, :nope]
        first = jnp.dot(two, wuk_ref[2 * pair], preferred_element_type=F32)
        second = jnp.dot(two, wuk_ref[2 * pair + 1], preferred_element_type=F32)
        parts += [first[:8], second[8:]]
    absorbed = jnp.concatenate(parts, 0)
    full_ref[...] = jnp.concatenate([absorbed, q[:, nope:].astype(F32)], -1).astype(BF16)


def main_kernel(
    scale,
    q_hbm,
    ka_hbm,
    kb_hbm,
    wuk_hbm,
    wuv_hbm,
    out_ref,
    q_ref,
    ka_ref,
    kb_ref,
    wuk_ref,
    wuv_ref,
    sems,
):
    copies = [
        pltpu.make_async_copy(source, target, sems.at[i])
        for i, (source, target) in enumerate(
            [
                (q_hbm, q_ref),
                (wuk_hbm.at[:2], wuk_ref.at[:2]),
                (ka_hbm, ka_ref),
                (wuk_hbm.at[2:], wuk_ref.at[2:]),
                (kb_hbm, kb_ref),
                (wuv_hbm, wuv_ref),
            ]
        )
    ]
    for copy in copies:
        copy.start()
    nope, latent = wuk_ref.shape[1:]

    def absorb(pair):
        both = q_ref[:, 16 * pair : 16 * pair + 16, :].astype(F32).reshape(CHIPS, 2, 8, -1)
        fulls = []
        for j in range(2):
            one = both[:, j].reshape(128, -1).astype(BF16)
            absorbed = jnp.dot(
                one[:, :nope], wuk_ref[2 * pair + j], preferred_element_type=F32
            ).astype(BF16)
            fulls.append(jnp.concatenate([absorbed, one[:, nope:]], -1))
        return fulls

    copies[0].wait()
    copies[1].wait()
    fulls = absorb(0)
    copies[2].wait()
    copies[3].wait()
    for pair in range(1, 4):
        fulls += absorb(pair)
    full = jnp.concatenate(fulls, 0)

    half = ka_ref.shape[1] // 2
    blocks = [(keys, i * half) for keys in (ka_ref, kb_ref) for i in range(2)]

    def score(keys, at):
        return jnp.dot(full, keys[:, at : at + half], preferred_element_type=F32)

    scores = score(*blocks[0])
    peak = None
    for i, (keys, at) in enumerate(blocks):
        if i == 0:
            copies[4].wait()
            copies[5].wait()
        later = score(*blocks[i + 1]) if i < 3 else None
        top = jnp.max(scores, -1, keepdims=True)
        top = top if peak is None else jnp.maximum(peak, top)
        expd = jnp.exp2((scores - top) * (scale * LOG2E))
        part = lax.dot_general(
            expd.astype(BF16), keys[:latent, at : at + half], NT, preferred_element_type=F32
        )
        if peak is None:
            mass, acc = jnp.sum(expd, -1, keepdims=True), part
        else:
            fade = jnp.exp2((peak - top) * (scale * LOG2E))
            mass = mass * fade + jnp.sum(expd, -1, keepdims=True)
            acc = acc * fade + part
        peak, scores = top, later

    attn = (acc / mass).astype(BF16)
    lane = lax.broadcasted_iota(jnp.int32, (128, 128), 1)
    stats = jnp.zeros((128, 128), F32)
    for pair in range(4):
        values = []
        for j in range(2):
            head = 2 * pair + j
            here = slice(128 * head, 128 * head + 128)
            values.append(
                jnp.dot(attn[here], wuv_ref[head], preferred_element_type=F32).reshape(
                    CHIPS, 8, 128
                )
            )
            for k, piece in enumerate(split3(peak[here]) + split3(mass[here])):
                stats = jnp.where(lane == 8 * k + head, piece, stats)
        out_ref[:, 16 * pair : 16 * pair + 16, :] = jnp.concatenate(values, 1).astype(BF16)
    stats = stats.reshape(CHIPS, 8, 128)
    out_ref[:, 64:80, :] = jnp.concatenate([stats, jnp.zeros_like(stats)], 1).astype(BF16)


def local_kernel(
    scale, full_ref, suffix_ref, lengths_ref, rope_ref, new_ref, wuv_ref, out_ref, stats_ref
):
    latent = wuv_ref.shape[1]
    full = full_ref[...]
    pieces = new_ref[...].astype(F32)
    lane = lax.broadcasted_iota(jnp.int32, (4, 128), 1) // 32
    parts = []
    for k in range(3):
        groups = []
        for g in range(4):
            group = 0.0
            for j in range(4):
                only = jnp.where(lane == k, pieces[4 * g + j], 0.0)
                shift = (32 * (j - k)) % 128
                group = group + (pltpu.roll(only, shift, 1) if shift else only)
            groups.append(group)
        parts.append(jnp.concatenate(groups, -1))
    new = jnp.concatenate(parts, 0)
    plain, gain = new[:8], new[8:9]
    square = jnp.sum(plain * plain, -1, keepdims=True) / latent
    normed = plain * lax.rsqrt(square + eps) * gain
    fresh = jnp.concatenate([normed, rope_ref[...].astype(F32)], -1)
    fresh = jnp.concatenate([fresh, jnp.zeros((120, fresh.shape[1]), F32)], 0).astype(BF16)

    gen = suffix_ref.shape[2]
    row = lax.broadcasted_iota(jnp.int32, (64, gen), 0) % 8
    col = lax.broadcasted_iota(jnp.int32, (64, gen), 1)
    scores, keys = [], []
    for sample in range(2):
        block = suffix_ref[sample]
        raw = jnp.dot(full, block, preferred_element_type=F32)
        live = (row // 4 == sample) & (col < lengths_ref[sample])
        scores.append(jnp.where(live, raw, -jnp.inf))
        keys.append(block[:latent])
    raw = lax.dot_general(full, fresh, NT, preferred_element_type=F32)
    row, col = row[:, :128], col[:, :128]
    live = (col < 8) & (col // 4 == row // 4) & (col <= row)
    scores.append(jnp.where(live, raw, -jnp.inf))
    keys.append(fresh[:, :latent].T)
    peak = functools.reduce(jnp.maximum, [jnp.max(s, -1, keepdims=True) for s in scores])
    mass, acc = 0.0, 0.0
    for s, v in zip(scores, keys):
        p = jnp.exp2((s - peak) * (scale * LOG2E))
        mass = mass + jnp.sum(p, -1, keepdims=True)
        acc = acc + lax.dot_general(p.astype(BF16), v, NT, preferred_element_type=F32)
    attn = (acc / mass).astype(BF16)
    lane = lax.broadcasted_iota(jnp.int32, (8, 128), 1)
    stats = jnp.zeros((8, 128), F32)
    for pair in range(4):
        two = attn[16 * pair : 16 * pair + 16]
        first = jnp.dot(two, wuv_ref[2 * pair], preferred_element_type=F32)
        second = jnp.dot(two, wuv_ref[2 * pair + 1], preferred_element_type=F32)
        out_ref[16 * pair : 16 * pair + 8, :] = first[:8]
        out_ref[16 * pair + 8 : 16 * pair + 16, :] = second[8:]
    for head in range(8):
        here = slice(8 * head, 8 * head + 8)
        stats = jnp.where(lane == head, peak[here], stats)
        stats = jnp.where(lane == 8 + head, mass[here], stats)
    stats_ref[...] = stats


def combine_kernel(scale, got_ref, own_ref, own_stats_ref, out_ref):
    raw = got_ref[:, 64:80, :].astype(F32)[:, :8, :].reshape(128, 128)

    def lanes(k):
        return raw if k == 0 else pltpu.roll(raw, 128 - 8 * k, 1)

    peaks = (lanes(0) + lanes(1) + lanes(2)).reshape(CHIPS, 8, 128)
    masses = (lanes(3) + lanes(4) + lanes(5)).reshape(CHIPS, 8, 128)
    own_peak = own_stats_ref[...]
    own_mass = pltpu.roll(own_peak, 128 - 8, 1)
    peak = jnp.maximum(jnp.max(peaks, 0), own_peak)
    weights = jnp.exp2((peaks - peak[None]) * (scale * LOG2E)) * masses
    own_weight = jnp.exp2((own_peak - peak) * (scale * LOG2E)) * own_mass
    inverse = 1.0 / (jnp.sum(weights, 0) + own_weight)
    for pair in range(4):
        got = got_ref[:, 16 * pair : 16 * pair + 16, :].astype(F32)
        for j in range(2):
            head = 2 * pair + j
            total = own_weight[:, head : head + 1] * own_ref[8 * head : 8 * head + 8, :]
            for chip in range(CHIPS):
                total = total + weights[chip, :, head : head + 1] * got[chip, 8 * j : 8 * j + 8, :]
            total = total * inverse[:, head : head + 1]
            out_ref[:, 128 * head : 128 * head + 128] = total.astype(BF16)


def call(kernel, outs, n_in, smem=(), hbm=(), scratch=(), cost=1, mib=24):
    spaces = [pltpu.SMEM if i in smem else pl.ANY if i in hbm else VMEM for i in range(n_in)]
    return pl.pallas_call(
        kernel,
        out_shape=outs,
        in_specs=[pl.BlockSpec(memory_space=space) for space in spaces],
        out_specs=jax.tree.map(lambda _: pl.BlockSpec(memory_space=VMEM), outs),
        scratch_shapes=scratch,
        compiler_params=pltpu.CompilerParams(vmem_limit_bytes=mib * 1024 * 1024),
        cost_estimate=pl.CostEstimate(
            flops=cost * 10**9, transcendentals=0, bytes_accessed=0
        ),
    )


def per_device(
    queries, prompt_cache, suffix_cache, gen_lengths, new_latent, new_rope, latent_gain, w_uk, w_uv
):
    width = queries.shape[2]
    scale = float(width) ** (-0.5)
    sent = call(queries_kernel, jax.ShapeDtypeStruct((CHIPS, 64, width), BF16), 1)(queries)
    mine, full = call(
        own_kernel,
        (
            jax.ShapeDtypeStruct((16, 4, 128), BF16),
            jax.ShapeDtypeStruct((64, prompt_cache.shape[1]), BF16),
        ),
        4,
        cost=30,
    )(sent, new_latent, latent_gain[None], w_uk)
    gathered = lax.all_to_all(sent, PLANE, 0, 0, tiled=True)
    keys = prompt_cache.T
    other = lax.ppermute(keys, "core", [(0, 1), (1, 0)])
    news = lax.all_to_all(mine, "z", 0, 0, tiled=True)
    parts = call(
        functools.partial(main_kernel, scale),
        jax.ShapeDtypeStruct((CHIPS, 80, 128), BF16),
        5,
        hbm=(0, 1, 2, 3, 4),
        scratch=[
            VMEM(gathered.shape, BF16),
            VMEM(keys.shape, BF16),
            VMEM(keys.shape, BF16),
            VMEM(w_uk.shape, BF16),
            VMEM(w_uv.shape, BF16),
            pltpu.SemaphoreType.DMA((6,)),
        ],
        cost=8,
        mib=59,
    )(gathered, keys, other, w_uk, w_uv)
    got = lax.all_to_all(parts, PLANE, 0, 0, tiled=True)
    own, own_stats = call(
        functools.partial(local_kernel, scale),
        (jax.ShapeDtypeStruct((64, 128), F32), jax.ShapeDtypeStruct((8, 128), F32)),
        6,
        smem=(2,),
    )(full, jnp.swapaxes(suffix_cache, 1, 2), gen_lengths, new_rope, news, w_uv)
    return call(
        functools.partial(combine_kernel, scale), jax.ShapeDtypeStruct((8, 1024), BF16), 3
    )(got, own, own_stats)


def solution(mesh):
    fine = Mesh(mesh.devices.reshape(4, 4, 2, 16), ("y", "x", "core", "z"))
    seq = ("y", "x", "core")
    return jax.shard_map(
        per_device,
        mesh=fine,
        in_specs=(
            P(seq, "z", None),
            P(seq, None),
            P(seq, None, None),
            P(seq),
            P(seq, "z"),
            P(seq, None),
            P("z"),
            P("z", None, None),
            P("z", None, None),
        ),
        out_specs=P(seq, "z"),
        check_vma=False,
    )
```

```python
import functools

import jax
import jax.numpy as jnp
from jax import lax
from jax.experimental import pallas as pl
from jax.experimental.pallas import tpu as pltpu
from jax.sharding import Mesh
from jax.sharding import PartitionSpec as P

eps = 1e-06
LOG2E = 1.4426950408889634
CHIPS = 16
PLANE = ("y", "x")
F32 = jnp.float32
BF16 = jnp.bfloat16
VMEM = pltpu.VMEM
NT = (((1,), (1,)), ((), ()))


def split3(value):
    high = value.astype(BF16).astype(F32)
    rest = value - high
    middle = rest.astype(BF16).astype(F32)
    return high, middle, (rest - middle).astype(BF16).astype(F32)


def queries_kernel(queries_ref, latent_ref, gain_ref, sent_ref):
    by_head = jnp.swapaxes(queries_ref[...].astype(F32), 0, 1)
    rows = by_head.reshape(64, by_head.shape[2])
    gain = jnp.concatenate([gain_ref[...].astype(F32), jnp.zeros((7, 32), F32)], 0)
    extra = jnp.concatenate([latent_ref[...].astype(F32), gain], 1)
    extra = jnp.concatenate([extra, jnp.zeros((56, 64), F32)], 0)
    rows = jnp.concatenate([rows, extra], 1).astype(BF16)
    for chip in range(CHIPS):
        sent_ref[chip] = rows


def own_kernel(width, q_ref, wuk_ref, full_ref):
    nope = wuk_ref.shape[1]
    q = q_ref[0]
    parts = []
    for pair in range(4):
        two = q[16 * pair : 16 * pair + 16, :nope]
        first = jnp.dot(two, wuk_ref[2 * pair], preferred_element_type=F32)
        second = jnp.dot(two, wuk_ref[2 * pair + 1], preferred_element_type=F32)
        parts += [first[:8], second[8:]]
    absorbed = jnp.concatenate(parts, 0)
    full_ref[...] = jnp.concatenate([absorbed, q[:, nope:width].astype(F32)], -1).astype(BF16)


def main_kernel(
    width,
    q_hbm,
    ka_hbm,
    kb_hbm,
    wuk_hbm,
    wuv_hbm,
    out_ref,
    stats_ref,
    q_ref,
    ka_ref,
    kb_ref,
    wuk_ref,
    wuv_ref,
    sems,
):
    scale = float(width) ** (-0.5)
    copies = [
        pltpu.make_async_copy(source, target, sems.at[i])
        for i, (source, target) in enumerate(
            [
                (q_hbm, q_ref),
                (wuk_hbm.at[:2], wuk_ref.at[:2]),
                (ka_hbm, ka_ref),
                (wuk_hbm.at[2:], wuk_ref.at[2:]),
                (kb_hbm, kb_ref),
                (wuv_hbm, wuv_ref),
            ]
        )
    ]
    for copy in copies:
        copy.start()
    nope, latent = wuk_ref.shape[1:]

    def absorb(pair):
        both = q_ref[:, 16 * pair : 16 * pair + 16, :].astype(F32).reshape(CHIPS, 2, 8, -1)
        fulls = []
        for j in range(2):
            one = both[:, j].reshape(128, -1).astype(BF16)
            absorbed = jnp.dot(
                one[:, :nope], wuk_ref[2 * pair + j], preferred_element_type=F32
            ).astype(BF16)
            fulls.append(jnp.concatenate([absorbed, one[:, nope:width]], -1))
        return fulls

    copies[0].wait()
    copies[1].wait()
    fulls = absorb(0)
    copies[2].wait()
    copies[3].wait()
    for pair in range(1, 4):
        fulls += absorb(pair)
    full = jnp.concatenate(fulls, 0)

    half = ka_ref.shape[1] // 2
    blocks = [(keys, i * half) for keys in (ka_ref, kb_ref) for i in range(2)]

    def score(keys, at):
        return jnp.dot(full, keys[:, at : at + half], preferred_element_type=F32)

    scores = score(*blocks[0])
    peak = None
    for i, (keys, at) in enumerate(blocks):
        if i == 0:
            copies[4].wait()
            copies[5].wait()
        later = score(*blocks[i + 1]) if i < 3 else None
        top = jnp.max(scores, -1, keepdims=True)
        top = top if peak is None else jnp.maximum(peak, top)
        expd = jnp.exp2((scores - top) * (scale * LOG2E))
        part = lax.dot_general(
            expd.astype(BF16), keys[:latent, at : at + half], NT, preferred_element_type=F32
        )
        if peak is None:
            mass, acc = jnp.sum(expd, -1, keepdims=True), part
        else:
            fade = jnp.exp2((peak - top) * (scale * LOG2E))
            mass = mass * fade + jnp.sum(expd, -1, keepdims=True)
            acc = acc * fade + part
        peak, scores = top, later

    attn = (acc / mass).astype(BF16)
    lane = lax.broadcasted_iota(jnp.int32, (128, 128), 1)
    stats = jnp.zeros((128, 128), F32)
    for pair in range(4):
        values = []
        for j in range(2):
            head = 2 * pair + j
            here = slice(128 * head, 128 * head + 128)
            values.append(
                jnp.dot(attn[here], wuv_ref[head], preferred_element_type=F32).reshape(
                    CHIPS, 8, 128
                )
            )
            for k, piece in enumerate(split3(peak[here]) + split3(mass[here])):
                stats = jnp.where(lane == 8 * k + head, piece, stats)
        out_ref[:, 16 * pair : 16 * pair + 16, :] = jnp.concatenate(values, 1).astype(BF16)
    stats_ref[...] = stats.reshape(CHIPS, 8, 128)


def attach_kernel(values_ref, stats_ref, moved_ref, out_ref):
    moved = moved_ref[...].astype(F32)[:, :8, :].reshape(128, 128)
    moved = pltpu.roll(moved, 64, 1).reshape(CHIPS, 8, 128)
    out_ref[:, :64, :] = values_ref[...]
    out_ref[:, 64:80, :] = jnp.concatenate([stats_ref[...], moved], 1).astype(BF16)


def attend(scale, full, blocks, wuv_ref):
    latent = wuv_ref.shape[1]
    scores = []
    for live, keys in blocks:
        raw = jnp.dot(full, keys, preferred_element_type=F32)
        scores.append(jnp.where(live, raw, -jnp.inf))
    peak = functools.reduce(jnp.maximum, [jnp.max(s, -1, keepdims=True) for s in scores])
    mass, acc = 0.0, 0.0
    for s, (_, keys) in zip(scores, blocks):
        p = jnp.exp2((s - peak) * (scale * LOG2E))
        mass = mass + jnp.sum(p, -1, keepdims=True)
        acc = acc + lax.dot_general(
            p.astype(BF16), keys[:latent], NT, preferred_element_type=F32
        )
    attn = (acc / mass).astype(BF16)
    lane = lax.broadcasted_iota(jnp.int32, (8, 128), 1)
    peaks = masses = jnp.zeros((8, 128), F32)
    values = []
    for pair in range(4):
        two = attn[16 * pair : 16 * pair + 16]
        first = jnp.dot(two, wuv_ref[2 * pair], preferred_element_type=F32)
        second = jnp.dot(two, wuv_ref[2 * pair + 1], preferred_element_type=F32)
        values += [first[:8], second[8:]]
    for head in range(8):
        here = slice(8 * head, 8 * head + 8)
        peaks = jnp.where(lane == head, peak[here], peaks)
        masses = jnp.where(lane == head, mass[here], masses)
    return values, peaks, masses


def suffix_kernel(scale, full_ref, suffix_ref, lengths_ref, wuv_ref, out_ref, stats_ref):
    gen = suffix_ref.shape[2]
    row = lax.broadcasted_iota(jnp.int32, (64, gen), 0) % 8
    col = lax.broadcasted_iota(jnp.int32, (64, gen), 1)
    blocks = [
        ((row // 4 == sample) & (col < lengths_ref[sample]), suffix_ref[sample])
        for sample in range(2)
    ]
    values, peaks, masses = attend(scale, full_ref[...], blocks, wuv_ref)
    out_ref[...] = jnp.concatenate(values, 0)
    stats_ref[...] = jnp.concatenate([peaks, masses], 0)


def combine_kernel(
    scale, got_ref, suffix_ref, suffix_stats_ref, full_ref, rope_ref, wuv_ref, out_ref
):
    place = lax.axis_index("z")
    lane = lax.broadcasted_iota(jnp.int32, (8, 128), 1) // 32
    latents, gains = [], []
    for g in range(4):
        latent, gain = 0.0, 0.0
        for j in range(4):
            chip = (place - (4 * g + j)) & 15
            piece = got_ref[chip, 64:80, :].astype(F32)[8:]
            one = jnp.where(lane == 0, piece, 0.0)
            latent = latent + (pltpu.roll(one, 32 * j, 1) if j else one)
            one = jnp.where(lane == 1, piece, 0.0)
            shift = (32 * (j - 1)) % 128
            gain = gain + (pltpu.roll(one, shift, 1) if shift else one)
        latents.append(latent)
        gains.append(gain)
    plain, gain = jnp.concatenate(latents, -1), jnp.concatenate(gains, -1)[:1]
    square = jnp.sum(plain * plain, -1, keepdims=True) / plain.shape[1]
    normed = plain * lax.rsqrt(square + eps) * gain
    fresh = jnp.concatenate([normed, rope_ref[...].astype(F32)], -1)
    fresh = jnp.concatenate([fresh, jnp.zeros((120, fresh.shape[1]), F32)], 0)
    row = lax.broadcasted_iota(jnp.int32, (64, 128), 0) % 8
    col = lax.broadcasted_iota(jnp.int32, (64, 128), 1)
    live = (col < 8) & (col // 4 == row // 4) & (col <= row)
    fresh_values, fresh_peak, fresh_mass = attend(
        scale, full_ref[...], [(live, fresh.T.astype(BF16))], wuv_ref
    )

    raw = got_ref[:, 64:80, :].astype(F32)[:, :8, :].reshape(128, 128)

    def lanes(k):
        return raw if k == 0 else pltpu.roll(raw, 128 - 8 * k, 1)

    peaks = (lanes(0) + lanes(1) + lanes(2)).reshape(CHIPS, 8, 128)
    masses = (lanes(3) + lanes(4) + lanes(5)).reshape(CHIPS, 8, 128)
    suffix_peak, suffix_mass = suffix_stats_ref[:8], suffix_stats_ref[8:]
    peak = jnp.maximum(jnp.max(peaks, 0), jnp.maximum(suffix_peak, fresh_peak))
    weights = jnp.exp2((peaks - peak[None]) * (scale * LOG2E)) * masses
    suffix_weight = jnp.exp2((suffix_peak - peak) * (scale * LOG2E)) * suffix_mass
    fresh_weight = jnp.exp2((fresh_peak - peak) * (scale * LOG2E)) * fresh_mass
    inverse = 1.0 / (jnp.sum(weights, 0) + suffix_weight + fresh_weight)
    for pair in range(4):
        got = got_ref[:, 16 * pair : 16 * pair + 16, :].astype(F32)
        for j in range(2):
            head = 2 * pair + j
            this = slice(head, head + 1)
            total = suffix_weight[:, this] * suffix_ref[8 * head : 8 * head + 8, :]
            total = total + fresh_weight[:, this] * fresh_values[head]
            for chip in range(CHIPS):
                total = total + weights[chip, :, this] * got[chip, 8 * j : 8 * j + 8, :]
            total = total * inverse[:, this]
            out_ref[:, 128 * head : 128 * head + 128] = total.astype(BF16)


def call(kernel, outs, n_in, smem=(), hbm=(), scratch=(), cost=1, mib=24):
    spaces = [pltpu.SMEM if i in smem else pl.ANY if i in hbm else VMEM for i in range(n_in)]
    return pl.pallas_call(
        kernel,
        out_shape=outs,
        in_specs=[pl.BlockSpec(memory_space=space) for space in spaces],
        out_specs=jax.tree.map(lambda _: pl.BlockSpec(memory_space=VMEM), outs),
        scratch_shapes=scratch,
        compiler_params=pltpu.CompilerParams(vmem_limit_bytes=mib * 1024 * 1024),
        cost_estimate=pl.CostEstimate(
            flops=cost * 10**9, transcendentals=0, bytes_accessed=0
        ),
    )


def per_device(
    queries, prompt_cache, suffix_cache, gen_lengths, new_latent, new_rope, latent_gain, w_uk, w_uv
):
    width = queries.shape[2]
    scale = float(width) ** (-0.5)
    sent = call(
        queries_kernel, jax.ShapeDtypeStruct((CHIPS, 64, 256), BF16), 3, mib=62
    )(queries, new_latent, latent_gain[None])
    gathered = lax.all_to_all(sent, PLANE, 0, 0, tiled=True)
    keys = prompt_cache.T
    other = lax.ppermute(keys, "core", [(0, 1), (1, 0)])
    full = call(
        functools.partial(own_kernel, width),
        jax.ShapeDtypeStruct((64, keys.shape[0]), BF16),
        2,
        cost=30,
    )(sent, w_uk)

    devices = [(p, core, z) for p in range(CHIPS) for core in range(2) for z in range(16)]
    moves = [
        ((2 * p + core) * 16 + z, (2 * p + core) * 16 + (z + p) % 16) for p, core, z in devices
    ]
    moved = lax.ppermute(gathered[:, :16, 128:], ("y", "x", "core", "z"), moves)

    values, stats = call(
        functools.partial(main_kernel, width),
        (
            jax.ShapeDtypeStruct((CHIPS, 64, 128), BF16),
            jax.ShapeDtypeStruct((CHIPS, 8, 128), F32),
        ),
        5,
        hbm=(0, 1, 2, 3, 4),
        scratch=[
            VMEM(gathered.shape, BF16),
            VMEM(keys.shape, BF16),
            VMEM(keys.shape, BF16),
            VMEM(w_uk.shape, BF16),
            VMEM(w_uv.shape, BF16),
            pltpu.SemaphoreType.DMA((6,)),
        ],
        cost=8,
        mib=52,
    )(gathered, keys, other, w_uk, w_uv)
    parts = call(attach_kernel, jax.ShapeDtypeStruct((CHIPS, 80, 128), BF16), 3)(
        values, stats, moved
    )
    got = lax.all_to_all(parts, PLANE, 0, 0, tiled=True)
    suffix, suffix_stats = call(
        functools.partial(suffix_kernel, scale),
        (jax.ShapeDtypeStruct((64, 128), F32), jax.ShapeDtypeStruct((16, 128), F32)),
        4,
        smem=(2,),
        cost=5,
    )(full, jnp.swapaxes(suffix_cache, 1, 2), gen_lengths, w_uv)
    return call(
        functools.partial(combine_kernel, scale), jax.ShapeDtypeStruct((8, 1024), BF16), 6
    )(got, suffix, suffix_stats, full, new_rope, w_uv)


def solution(mesh):
    fine = Mesh(mesh.devices.reshape(4, 4, 2, 16), ("y", "x", "core", "z"))
    seq = ("y", "x", "core")
    return jax.shard_map(
        per_device,
        mesh=fine,
        in_specs=(
            P(seq, "z", None),
            P(seq, None),
            P(seq, None, None),
            P(seq),
            P(seq, "z"),
            P(seq, None),
            P("z"),
            P("z", None, None),
            P("z", None, None),
        ),
        out_specs=P(seq, "z"),
        check_vma=False,
    )
```

```python
import functools

import jax
import jax.numpy as jnp
from jax import lax
from jax.experimental import pallas as pl
from jax.experimental.pallas import tpu as pltpu
from jax.sharding import Mesh
from jax.sharding import PartitionSpec as P

eps = 1e-06
LOG2E = 1.4426950408889634
CHIPS = 16
PLANE = ("y", "x")
ORDER = sorted(
    range(CHIPS), key=lambda p: (abs(p // 4 - 2) + min((p - 2) % 4, (2 - p) % 4), p)
)
F32 = jnp.float32
BF16 = jnp.bfloat16
VMEM = pltpu.VMEM
NT = (((1,), (1,)), ((), ()))


def split3(value):
    high = value.astype(BF16).astype(F32)
    rest = value - high
    middle = rest.astype(BF16).astype(F32)
    return high, middle, (rest - middle).astype(BF16).astype(F32)


def queries_kernel(queries_ref, latent_ref, gain_ref, sent_ref):
    by_head = jnp.swapaxes(queries_ref[...].astype(F32), 0, 1)
    rows = by_head.reshape(64, by_head.shape[2])
    gain = jnp.concatenate([gain_ref[...].astype(F32), jnp.zeros((7, 32), F32)], 0)
    extra = jnp.concatenate([latent_ref[...].astype(F32), gain], 1)
    extra = jnp.concatenate([extra, jnp.zeros((56, 64), F32)], 0)
    rows = jnp.concatenate([rows, extra], 1).astype(BF16)
    for chip in range(CHIPS):
        sent_ref[chip] = rows


def own_kernel(width, q_ref, wuk_ref, full_ref):
    nope = wuk_ref.shape[1]
    q = q_ref[0]
    parts = []
    for pair in range(4):
        two = q[16 * pair : 16 * pair + 16, :nope]
        first = jnp.dot(two, wuk_ref[2 * pair], preferred_element_type=F32)
        second = jnp.dot(two, wuk_ref[2 * pair + 1], preferred_element_type=F32)
        parts += [first[:8], second[8:]]
    absorbed = jnp.concatenate(parts, 0)
    full_ref[...] = jnp.concatenate([absorbed, q[:, nope:width].astype(F32)], -1).astype(BF16)


def main_kernel(
    width,
    q_hbm,
    ka_hbm,
    kb_hbm,
    wuk_hbm,
    wuv_hbm,
    out_ref,
    stats_ref,
    q_ref,
    ka_ref,
    kb_ref,
    wuk_ref,
    wuv_ref,
    sems,
):
    scale = float(width) ** (-0.5)
    copies = [
        pltpu.make_async_copy(source, target, sems.at[i])
        for i, (source, target) in enumerate(
            [
                (q_hbm, q_ref),
                (wuk_hbm.at[:2], wuk_ref.at[:2]),
                (ka_hbm, ka_ref),
                (wuk_hbm.at[2:], wuk_ref.at[2:]),
                (kb_hbm, kb_ref),
                (wuv_hbm, wuv_ref),
            ]
        )
    ]
    for copy in copies:
        copy.start()
    nope, latent = wuk_ref.shape[1:]

    def absorb(pair):
        both = q_ref[:, 16 * pair : 16 * pair + 16, :].astype(F32).reshape(CHIPS, 2, 8, -1)
        fulls = []
        for j in range(2):
            one = both[:, j].reshape(128, -1).astype(BF16)
            absorbed = jnp.dot(
                one[:, :nope], wuk_ref[2 * pair + j], preferred_element_type=F32
            ).astype(BF16)
            fulls.append(jnp.concatenate([absorbed, one[:, nope:width]], -1))
        return fulls

    copies[0].wait()
    copies[1].wait()
    fulls = absorb(0)
    copies[2].wait()
    copies[3].wait()
    for pair in range(1, 4):
        fulls += absorb(pair)
    full = jnp.concatenate(fulls, 0)

    half = ka_ref.shape[1] // 2
    blocks = [(keys, i * half) for keys in (ka_ref, kb_ref) for i in range(2)]

    def score(keys, at):
        return jnp.dot(full, keys[:, at : at + half], preferred_element_type=F32)

    scores = score(*blocks[0])
    peak = None
    for i, (keys, at) in enumerate(blocks):
        if i == 0:
            copies[4].wait()
            copies[5].wait()
        later = score(*blocks[i + 1]) if i < 3 else None
        top = jnp.max(scores, -1, keepdims=True)
        top = top if peak is None else jnp.maximum(peak, top)
        expd = jnp.exp2((scores - top) * (scale * LOG2E))
        part = lax.dot_general(
            expd.astype(BF16), keys[:latent, at : at + half], NT, preferred_element_type=F32
        )
        if peak is None:
            mass, acc = jnp.sum(expd, -1, keepdims=True), part
        else:
            fade = jnp.exp2((peak - top) * (scale * LOG2E))
            mass = mass * fade + jnp.sum(expd, -1, keepdims=True)
            acc = acc * fade + part
        peak, scores = top, later

    attn = (acc / mass).astype(BF16)
    lane = lax.broadcasted_iota(jnp.int32, (128, 128), 1)
    stats = jnp.zeros((128, 128), F32)
    for pair in range(4):
        values = []
        for j in range(2):
            head = 2 * pair + j
            here = slice(128 * head, 128 * head + 128)
            values.append(
                jnp.dot(attn[here], wuv_ref[head], preferred_element_type=F32).reshape(
                    CHIPS, 8, 128
                )
            )
            for k, piece in enumerate(split3(peak[here]) + split3(mass[here])):
                stats = jnp.where(lane == 8 * k + head, piece, stats)
        out_ref[:, 16 * pair : 16 * pair + 16, :] = jnp.concatenate(values, 1).astype(BF16)
    stats_ref[...] = stats.reshape(CHIPS, 8, 128)


def attach_kernel(values_ref, stats_ref, moved_ref, out_ref):
    moved = moved_ref[...].astype(F32)[:, :8, :].reshape(128, 128)
    moved = pltpu.roll(moved, 64, 1).reshape(CHIPS, 8, 128)
    out_ref[:, :64, :] = values_ref[...]
    out_ref[:, 64:80, :] = jnp.concatenate([stats_ref[...], moved], 1).astype(BF16)


def attend(scale, full, blocks, wuv_ref):
    latent = wuv_ref.shape[1]
    scores = []
    for live, keys in blocks:
        raw = jnp.dot(full, keys, preferred_element_type=F32)
        scores.append(jnp.where(live, raw, -jnp.inf))
    peak = functools.reduce(jnp.maximum, [jnp.max(s, -1, keepdims=True) for s in scores])
    mass, acc = 0.0, 0.0
    for s, (_, keys) in zip(scores, blocks):
        p = jnp.exp2((s - peak) * (scale * LOG2E))
        mass = mass + jnp.sum(p, -1, keepdims=True)
        acc = acc + lax.dot_general(
            p.astype(BF16), keys[:latent], NT, preferred_element_type=F32
        )
    attn = (acc / mass).astype(BF16)
    lane = lax.broadcasted_iota(jnp.int32, (8, 128), 1)
    peaks = masses = jnp.zeros((8, 128), F32)
    values = []
    for pair in range(4):
        two = attn[16 * pair : 16 * pair + 16]
        first = jnp.dot(two, wuv_ref[2 * pair], preferred_element_type=F32)
        second = jnp.dot(two, wuv_ref[2 * pair + 1], preferred_element_type=F32)
        values += [first[:8], second[8:]]
    for head in range(8):
        here = slice(8 * head, 8 * head + 8)
        peaks = jnp.where(lane == head, peak[here], peaks)
        masses = jnp.where(lane == head, mass[here], masses)
    return values, peaks, masses


def suffix_kernel(scale, full_ref, suffix_ref, lengths_ref, wuv_ref, out_ref, stats_ref):
    gen = suffix_ref.shape[2]
    row = lax.broadcasted_iota(jnp.int32, (64, gen), 0) % 8
    col = lax.broadcasted_iota(jnp.int32, (64, gen), 1)
    blocks = [
        ((row // 4 == sample) & (col < lengths_ref[sample]), suffix_ref[sample])
        for sample in range(2)
    ]
    values, peaks, masses = attend(scale, full_ref[...], blocks, wuv_ref)
    out_ref[...] = jnp.concatenate(values, 0)
    stats_ref[...] = jnp.concatenate([peaks, masses], 0)


def combine_kernel(
    scale, got_ref, suffix_ref, suffix_stats_ref, full_ref, rope_ref, wuv_ref, out_ref
):
    place = lax.axis_index("z")
    lane = lax.broadcasted_iota(jnp.int32, (8, 128), 1) // 32
    latents, gains = [], []
    for g in range(4):
        latent, gain = 0.0, 0.0
        for j in range(4):
            chip = ((place - (4 * g + j)) & 15) ^ 8
            piece = got_ref[chip, 64:80, :].astype(F32)[8:]
            one = jnp.where(lane == 0, piece, 0.0)
            latent = latent + (pltpu.roll(one, 32 * j, 1) if j else one)
            one = jnp.where(lane == 1, piece, 0.0)
            shift = (32 * (j - 1)) % 128
            gain = gain + (pltpu.roll(one, shift, 1) if shift else one)
        latents.append(latent)
        gains.append(gain)
    plain, gain = jnp.concatenate(latents, -1), jnp.concatenate(gains, -1)[:1]
    square = jnp.sum(plain * plain, -1, keepdims=True) / plain.shape[1]
    normed = plain * lax.rsqrt(square + eps) * gain
    fresh = jnp.concatenate([normed, rope_ref[...].astype(F32)], -1)
    fresh = jnp.concatenate([fresh, jnp.zeros((120, fresh.shape[1]), F32)], 0)
    row = lax.broadcasted_iota(jnp.int32, (64, 128), 0) % 8
    col = lax.broadcasted_iota(jnp.int32, (64, 128), 1)
    live = (col < 8) & (col // 4 == row // 4) & (col <= row)
    fresh_values, fresh_peak, fresh_mass = attend(
        scale, full_ref[...], [(live, fresh.T.astype(BF16))], wuv_ref
    )

    raw = got_ref[:, 64:80, :].astype(F32)[:, :8, :].reshape(128, 128)

    def lanes(k):
        return raw if k == 0 else pltpu.roll(raw, 128 - 8 * k, 1)

    peaks = (lanes(0) + lanes(1) + lanes(2)).reshape(CHIPS, 8, 128)
    masses = (lanes(3) + lanes(4) + lanes(5)).reshape(CHIPS, 8, 128)
    suffix_peak, suffix_mass = suffix_stats_ref[:8], suffix_stats_ref[8:]
    peak = jnp.maximum(jnp.max(peaks, 0), jnp.maximum(suffix_peak, fresh_peak))
    weights = jnp.exp2((peaks - peak[None]) * (scale * LOG2E)) * masses
    suffix_weight = jnp.exp2((suffix_peak - peak) * (scale * LOG2E)) * suffix_mass
    fresh_weight = jnp.exp2((fresh_peak - peak) * (scale * LOG2E)) * fresh_mass
    inverse = 1.0 / (jnp.sum(weights, 0) + suffix_weight + fresh_weight)
    for pair in range(4):
        got = got_ref[:, 16 * pair : 16 * pair + 16, :].astype(F32)
        for j in range(2):
            head = 2 * pair + j
            this = slice(head, head + 1)
            total = suffix_weight[:, this] * suffix_ref[8 * head : 8 * head + 8, :]
            total = total + fresh_weight[:, this] * fresh_values[head]
            for chip in range(CHIPS):
                total = total + weights[chip, :, this] * got[chip, 8 * j : 8 * j + 8, :]
            total = total * inverse[:, this]
            out_ref[:, 128 * head : 128 * head + 128] = total.astype(BF16)


def call(kernel, outs, n_in, smem=(), hbm=(), scratch=(), cost=1, mib=24):
    spaces = [pltpu.SMEM if i in smem else pl.ANY if i in hbm else VMEM for i in range(n_in)]
    return pl.pallas_call(
        kernel,
        out_shape=outs,
        in_specs=[pl.BlockSpec(memory_space=space) for space in spaces],
        out_specs=jax.tree.map(lambda _: pl.BlockSpec(memory_space=VMEM), outs),
        scratch_shapes=scratch,
        compiler_params=pltpu.CompilerParams(vmem_limit_bytes=mib * 1024 * 1024),
        cost_estimate=pl.CostEstimate(
            flops=cost * 10**9, transcendentals=0, bytes_accessed=0
        ),
    )


def per_device(
    queries, prompt_cache, suffix_cache, gen_lengths, new_latent, new_rope, latent_gain, w_uk, w_uv
):
    width = queries.shape[2]
    scale = float(width) ** (-0.5)
    sent = call(
        queries_kernel, jax.ShapeDtypeStruct((CHIPS, 64, 256), BF16), 3, mib=62
    )(queries, new_latent, latent_gain[None])
    gathered = lax.all_to_all(sent, PLANE, 0, 0, axis_index_groups=[ORDER], tiled=True)
    keys = prompt_cache.T
    other = lax.ppermute(keys, "core", [(0, 1), (1, 0)])
    full = call(
        functools.partial(own_kernel, width),
        jax.ShapeDtypeStruct((64, keys.shape[0]), BF16),
        2,
        cost=30,
    )(sent, w_uk)

    moves = [
        ((2 * p + core) * 16 + z, (2 * p + core) * 16 + (z + (8 ^ k)) % 16)
        for k, p in enumerate(ORDER)
        for core in range(2)
        for z in range(16)
    ]
    moved = lax.ppermute(gathered[:, :16, 128:], ("y", "x", "core", "z"), moves)

    values, stats = call(
        functools.partial(main_kernel, width),
        (
            jax.ShapeDtypeStruct((CHIPS, 64, 128), BF16),
            jax.ShapeDtypeStruct((CHIPS, 8, 128), F32),
        ),
        5,
        hbm=(0, 1, 2, 3, 4),
        scratch=[
            VMEM(gathered.shape, BF16),
            VMEM(keys.shape, BF16),
            VMEM(keys.shape, BF16),
            VMEM(w_uk.shape, BF16),
            VMEM(w_uv.shape, BF16),
            pltpu.SemaphoreType.DMA((6,)),
        ],
        cost=8,
        mib=52,
    )(gathered, keys, other, w_uk, w_uv)
    parts = call(attach_kernel, jax.ShapeDtypeStruct((CHIPS, 80, 128), BF16), 3)(
        values, stats, moved
    )
    got = lax.all_to_all(parts, PLANE, 0, 0, axis_index_groups=[ORDER], tiled=True)
    suffix, suffix_stats = call(
        functools.partial(suffix_kernel, scale),
        (jax.ShapeDtypeStruct((64, 128), F32), jax.ShapeDtypeStruct((16, 128), F32)),
        4,
        smem=(2,),
        cost=5,
    )(full, jnp.swapaxes(suffix_cache, 1, 2), gen_lengths, w_uv)
    return call(
        functools.partial(combine_kernel, scale), jax.ShapeDtypeStruct((8, 1024), BF16), 6
    )(got, suffix, suffix_stats, full, new_rope, w_uv)


def solution(mesh):
    fine = Mesh(mesh.devices.reshape(4, 4, 2, 16), ("y", "x", "core", "z"))
    seq = ("y", "x", "core")
    return jax.shard_map(
        per_device,
        mesh=fine,
        in_specs=(
            P(seq, "z", None),
            P(seq, None),
            P(seq, None, None),
            P(seq),
            P(seq, "z"),
            P(seq, None),
            P("z"),
            P("z", None, None),
            P("z", None, None),
        ),
        out_specs=P(seq, "z"),
        check_vma=False,
    )
```

```python
import functools

import jax
import jax.numpy as jnp
from jax import lax
from jax.experimental import pallas as pl
from jax.experimental.pallas import tpu as pltpu
from jax.sharding import Mesh
from jax.sharding import PartitionSpec as P

eps = 1e-06
LOG2E = 1.4426950408889634
CHIPS = 16
PLANE = ("y", "x")
ORDER = sorted(
    range(CHIPS), key=lambda p: (abs(p // 4 - 2) + min((p - 2) % 4, (2 - p) % 4), p)
)
F32 = jnp.float32
BF16 = jnp.bfloat16
VMEM = pltpu.VMEM
NT = (((1,), (1,)), ((), ()))


def split3(value):
    high = value.astype(BF16).astype(F32)
    rest = value - high
    middle = rest.astype(BF16).astype(F32)
    return high, middle, (rest - middle).astype(BF16).astype(F32)


def queries_kernel(nope, queries_ref, latent_ref, gain_ref, sent_hbm, tile_ref, sems):
    by_head = jnp.swapaxes(queries_ref[...].astype(F32), 0, 1)
    rows = by_head.reshape(64, by_head.shape[2])
    rotated = jnp.concatenate([rows[:32, nope:], rows[32:, nope:]], 1)
    gain = jnp.concatenate([gain_ref[...].astype(F32), jnp.zeros((7, 32), F32)], 0)
    extra = jnp.concatenate([latent_ref[...].astype(F32), gain, jnp.zeros((8, 64), F32)], 1)
    extra = jnp.concatenate([extra, jnp.zeros((8, 128), F32)], 0)
    tile_ref[...] = jnp.concatenate([rows[:, :nope], rotated, extra], 0).astype(BF16)
    copies = [
        pltpu.make_async_copy(tile_ref, sent_hbm.at[chip], sems.at[chip]) for chip in range(CHIPS)
    ]
    for copy in copies:
        copy.start()
    for copy in copies:
        copy.wait()


def own_kernel(q_ref, wuk_ref, full_ref):
    q = q_ref[0]
    parts = []
    for pair in range(4):
        two = q[16 * pair : 16 * pair + 16]
        first = jnp.dot(two, wuk_ref[2 * pair], preferred_element_type=F32)
        second = jnp.dot(two, wuk_ref[2 * pair + 1], preferred_element_type=F32)
        parts += [first[:8], second[8:]]
    absorbed = jnp.concatenate(parts, 0)
    rotated = q[64:96].astype(F32)
    rotated = jnp.concatenate([rotated[:, :64], rotated[:, 64:]], 0)
    full_ref[...] = jnp.concatenate([absorbed, rotated], -1).astype(BF16)


def main_kernel(
    width,
    q_hbm,
    ka_hbm,
    kb_hbm,
    wuk_hbm,
    wuv_hbm,
    out_ref,
    stats_ref,
    q_ref,
    ka_ref,
    kb_ref,
    wuk_ref,
    wuv_ref,
    sems,
):
    scale = float(width) ** (-0.5)
    copies = [
        pltpu.make_async_copy(source, target, sems.at[i])
        for i, (source, target) in enumerate(
            [
                (q_hbm, q_ref),
                (wuk_hbm.at[:2], wuk_ref.at[:2]),
                (ka_hbm, ka_ref),
                (wuk_hbm.at[2:], wuk_ref.at[2:]),
                (kb_hbm, kb_ref),
                (wuv_hbm, wuv_ref),
            ]
        )
    ]
    for copy in copies:
        copy.start()
    latent = wuk_ref.shape[2]

    def absorb(pair):
        both = q_ref[:, 16 * pair : 16 * pair + 16, :].astype(F32).reshape(CHIPS, 2, 8, -1)
        top, side = 64 + 16 * (pair % 2), 64 * (pair // 2)
        rotated = q_ref[:, top : top + 16, :].astype(F32)[:, :, side : side + 64]
        rotated = rotated.reshape(CHIPS, 2, 8, -1)
        fulls = []
        for j in range(2):
            one = both[:, j].reshape(128, -1).astype(BF16)
            absorbed = jnp.dot(one, wuk_ref[2 * pair + j], preferred_element_type=F32)
            last = rotated[:, j].reshape(128, -1)
            fulls.append(jnp.concatenate([absorbed, last], -1).astype(BF16))
        return fulls

    copies[0].wait()
    copies[1].wait()
    fulls = absorb(0)
    copies[2].wait()
    copies[3].wait()
    for pair in range(1, 4):
        fulls += absorb(pair)
    full = jnp.concatenate(fulls, 0)

    half = ka_ref.shape[1] // 2
    blocks = [(keys, i * half) for keys in (ka_ref, kb_ref) for i in range(2)]

    def score(keys, at):
        return jnp.dot(full, keys[:, at : at + half], preferred_element_type=F32)

    scores = score(*blocks[0])
    peak = None
    for i, (keys, at) in enumerate(blocks):
        if i == 0:
            copies[4].wait()
            copies[5].wait()
        later = score(*blocks[i + 1]) if i < 3 else None
        top = jnp.max(scores, -1, keepdims=True)
        top = top if peak is None else jnp.maximum(peak, top)
        expd = jnp.exp2((scores - top) * (scale * LOG2E))
        part = lax.dot_general(
            expd.astype(BF16), keys[:latent, at : at + half], NT, preferred_element_type=F32
        )
        if peak is None:
            mass, acc = jnp.sum(expd, -1, keepdims=True), part
        else:
            fade = jnp.exp2((peak - top) * (scale * LOG2E))
            mass = mass * fade + jnp.sum(expd, -1, keepdims=True)
            acc = acc * fade + part
        peak, scores = top, later

    attn = (acc / mass).astype(BF16)
    lane = lax.broadcasted_iota(jnp.int32, (128, 128), 1)
    stats = jnp.zeros((128, 128), F32)
    for pair in range(4):
        values = []
        for j in range(2):
            head = 2 * pair + j
            here = slice(128 * head, 128 * head + 128)
            values.append(
                jnp.dot(attn[here], wuv_ref[head], preferred_element_type=F32).reshape(
                    CHIPS, 8, 128
                )
            )
            for k, piece in enumerate(split3(peak[here]) + split3(mass[here])):
                stats = jnp.where(lane == 8 * k + head, piece, stats)
        out_ref[:, 16 * pair : 16 * pair + 16, :] = jnp.concatenate(values, 1).astype(BF16)
    stats_ref[...] = stats.reshape(CHIPS, 8, 128)


def attach_kernel(values_ref, stats_ref, moved_ref, out_ref):
    moved = moved_ref[...].astype(F32)[:, :8, :]
    out_ref[:, :64, :] = values_ref[...]
    out_ref[:, 64:80, :] = jnp.concatenate([stats_ref[...], moved], 1).astype(BF16)


def attend(scale, full, blocks, wuv_ref):
    latent = wuv_ref.shape[1]
    scores = []
    for live, keys in blocks:
        raw = jnp.dot(full, keys, preferred_element_type=F32)
        scores.append(jnp.where(live, raw, -jnp.inf))
    peak = functools.reduce(jnp.maximum, [jnp.max(s, -1, keepdims=True) for s in scores])
    mass, acc = 0.0, 0.0
    for s, (_, keys) in zip(scores, blocks):
        p = jnp.exp2((s - peak) * (scale * LOG2E))
        mass = mass + jnp.sum(p, -1, keepdims=True)
        acc = acc + lax.dot_general(
            p.astype(BF16), keys[:latent], NT, preferred_element_type=F32
        )
    attn = (acc / mass).astype(BF16)
    lane = lax.broadcasted_iota(jnp.int32, (8, 128), 1)
    peaks = masses = jnp.zeros((8, 128), F32)
    values = []
    for pair in range(4):
        two = attn[16 * pair : 16 * pair + 16]
        first = jnp.dot(two, wuv_ref[2 * pair], preferred_element_type=F32)
        second = jnp.dot(two, wuv_ref[2 * pair + 1], preferred_element_type=F32)
        values += [first[:8], second[8:]]
    for head in range(8):
        here = slice(8 * head, 8 * head + 8)
        peaks = jnp.where(lane == head, peak[here], peaks)
        masses = jnp.where(lane == head, mass[here], masses)
    return values, peaks, masses


def suffix_kernel(scale, full_ref, suffix_ref, lengths_ref, wuv_ref, out_ref, stats_ref):
    gen = suffix_ref.shape[2]
    row = lax.broadcasted_iota(jnp.int32, (64, gen), 0) % 8
    col = lax.broadcasted_iota(jnp.int32, (64, gen), 1)
    blocks = [
        ((row // 4 == sample) & (col < lengths_ref[sample]), suffix_ref[sample])
        for sample in range(2)
    ]
    values, peaks, masses = attend(scale, full_ref[...], blocks, wuv_ref)
    out_ref[...] = jnp.concatenate(values, 0)
    stats_ref[...] = jnp.concatenate([peaks, masses], 0)


def combine_kernel(
    scale, got_ref, suffix_ref, suffix_stats_ref, full_ref, rope_ref, wuv_ref, out_ref
):
    place = lax.axis_index("z")
    lane = lax.broadcasted_iota(jnp.int32, (8, 128), 1) // 32
    latents, gains = [], []
    for g in range(4):
        latent, gain = 0.0, 0.0
        for j in range(4):
            chip = ((place - (4 * g + j)) & 15) ^ 8
            piece = got_ref[chip, 64:80, :].astype(F32)[8:]
            one = jnp.where(lane == 0, piece, 0.0)
            latent = latent + (pltpu.roll(one, 32 * j, 1) if j else one)
            one = jnp.where(lane == 1, piece, 0.0)
            shift = (32 * (j - 1)) % 128
            gain = gain + (pltpu.roll(one, shift, 1) if shift else one)
        latents.append(latent)
        gains.append(gain)
    plain, gain = jnp.concatenate(latents, -1), jnp.concatenate(gains, -1)[:1]
    square = jnp.sum(plain * plain, -1, keepdims=True) / plain.shape[1]
    normed = plain * lax.rsqrt(square + eps) * gain
    fresh = jnp.concatenate([normed, rope_ref[...].astype(F32)], -1)
    fresh = jnp.concatenate([fresh, jnp.zeros((120, fresh.shape[1]), F32)], 0)
    row = lax.broadcasted_iota(jnp.int32, (64, 128), 0) % 8
    col = lax.broadcasted_iota(jnp.int32, (64, 128), 1)
    live = (col < 8) & (col // 4 == row // 4) & (col <= row)
    fresh_values, fresh_peak, fresh_mass = attend(
        scale, full_ref[...], [(live, fresh.T.astype(BF16))], wuv_ref
    )

    raw = got_ref[:, 64:80, :].astype(F32)[:, :8, :].reshape(128, 128)

    def lanes(k):
        return raw if k == 0 else pltpu.roll(raw, 128 - 8 * k, 1)

    peaks = (lanes(0) + lanes(1) + lanes(2)).reshape(CHIPS, 8, 128)
    masses = (lanes(3) + lanes(4) + lanes(5)).reshape(CHIPS, 8, 128)
    suffix_peak, suffix_mass = suffix_stats_ref[:8], suffix_stats_ref[8:]
    peak = jnp.maximum(jnp.max(peaks, 0), jnp.maximum(suffix_peak, fresh_peak))
    weights = jnp.exp2((peaks - peak[None]) * (scale * LOG2E)) * masses
    suffix_weight = jnp.exp2((suffix_peak - peak) * (scale * LOG2E)) * suffix_mass
    fresh_weight = jnp.exp2((fresh_peak - peak) * (scale * LOG2E)) * fresh_mass
    inverse = 1.0 / (jnp.sum(weights, 0) + suffix_weight + fresh_weight)
    for pair in range(4):
        got = got_ref[:, 16 * pair : 16 * pair + 16, :].astype(F32)
        for j in range(2):
            head = 2 * pair + j
            this = slice(head, head + 1)
            total = suffix_weight[:, this] * suffix_ref[8 * head : 8 * head + 8, :]
            total = total + fresh_weight[:, this] * fresh_values[head]
            for chip in range(CHIPS):
                total = total + weights[chip, :, this] * got[chip, 8 * j : 8 * j + 8, :]
            total = total * inverse[:, this]
            out_ref[:, 128 * head : 128 * head + 128] = total.astype(BF16)


def call(kernel, outs, n_in, smem=(), hbm=(), scratch=(), cost=1, mib=24):
    spaces = [pltpu.SMEM if i in smem else pl.ANY if i in hbm else VMEM for i in range(n_in)]
    return pl.pallas_call(
        kernel,
        out_shape=outs,
        in_specs=[pl.BlockSpec(memory_space=space) for space in spaces],
        out_specs=jax.tree.map(lambda _: pl.BlockSpec(memory_space=VMEM), outs),
        scratch_shapes=scratch,
        compiler_params=pltpu.CompilerParams(vmem_limit_bytes=mib * 1024 * 1024),
        cost_estimate=pl.CostEstimate(
            flops=cost * 10**9, transcendentals=0, bytes_accessed=0
        ),
    )


def per_device(
    queries, prompt_cache, suffix_cache, gen_lengths, new_latent, new_rope, latent_gain, w_uk, w_uv
):
    width = queries.shape[2]
    scale = float(width) ** (-0.5)
    sent = pl.pallas_call(
        functools.partial(queries_kernel, w_uk.shape[1]),
        out_shape=jax.ShapeDtypeStruct((CHIPS, 112, 128), BF16),
        in_specs=[pl.BlockSpec(memory_space=VMEM)] * 3,
        out_specs=pl.BlockSpec(memory_space=pl.ANY),
        scratch_shapes=[VMEM((112, 128), BF16), pltpu.SemaphoreType.DMA((CHIPS,))],
        compiler_params=pltpu.CompilerParams(vmem_limit_bytes=62 * 1024 * 1024),
    )(queries, new_latent, latent_gain[None])
    gathered = lax.all_to_all(sent, PLANE, 0, 0, axis_index_groups=[ORDER], tiled=True)
    keys = prompt_cache.T
    other = lax.ppermute(keys, "core", [(0, 1), (1, 0)])
    full = call(
        own_kernel,
        jax.ShapeDtypeStruct((64, keys.shape[0]), BF16),
        2,
        cost=30,
    )(sent, w_uk)

    moves = [
        ((2 * p + core) * 16 + z, (2 * p + core) * 16 + (z + (8 ^ k)) % 16)
        for k, p in enumerate(ORDER)
        for core in range(2)
        for z in range(16)
    ]
    moved = lax.ppermute(gathered[:, 96:, :], ("y", "x", "core", "z"), moves)

    values, stats = call(
        functools.partial(main_kernel, width),
        (
            jax.ShapeDtypeStruct((CHIPS, 64, 128), BF16),
            jax.ShapeDtypeStruct((CHIPS, 8, 128), F32),
        ),
        5,
        hbm=(0, 1, 2, 3, 4),
        scratch=[
            VMEM(gathered.shape, BF16),
            VMEM(keys.shape, BF16),
            VMEM(keys.shape, BF16),
            VMEM(w_uk.shape, BF16),
            VMEM(w_uv.shape, BF16),
            pltpu.SemaphoreType.DMA((6,)),
        ],
        cost=8,
        mib=52,
    )(gathered, keys, other, w_uk, w_uv)
    parts = call(attach_kernel, jax.ShapeDtypeStruct((CHIPS, 80, 128), BF16), 3)(
        values, stats, moved
    )
    got = lax.all_to_all(parts, PLANE, 0, 0, axis_index_groups=[ORDER], tiled=True)
    suffix, suffix_stats = call(
        functools.partial(suffix_kernel, scale),
        (jax.ShapeDtypeStruct((64, 128), F32), jax.ShapeDtypeStruct((16, 128), F32)),
        4,
        smem=(2,),
        cost=5,
    )(full, jnp.swapaxes(suffix_cache, 1, 2), gen_lengths, w_uv)
    return call(
        functools.partial(combine_kernel, scale), jax.ShapeDtypeStruct((8, 1024), BF16), 6
    )(got, suffix, suffix_stats, full, new_rope, w_uv)


def solution(mesh):
    fine = Mesh(mesh.devices.reshape(4, 4, 2, 16), ("y", "x", "core", "z"))
    seq = ("y", "x", "core")
    return jax.shard_map(
        per_device,
        mesh=fine,
        in_specs=(
            P(seq, "z", None),
            P(seq, None),
            P(seq, None, None),
            P(seq),
            P(seq, "z"),
            P(seq, None),
            P("z"),
            P("z", None, None),
            P("z", None, None),
        ),
        out_specs=P(seq, "z"),
        check_vma=False,
    )
```

```python
import functools

import jax
import jax.numpy as jnp
from jax import lax
from jax.experimental import pallas as pl
from jax.experimental.pallas import tpu as pltpu
from jax.sharding import Mesh
from jax.sharding import PartitionSpec as P

eps = 1e-06
LOG2E = 1.4426950408889634
CHIPS = 16
PLANE = ("y", "x")
ORDER = sorted(
    range(CHIPS), key=lambda p: (abs(p // 4 - 2) + min((p - 2) % 4, (2 - p) % 4), p)
)
F32 = jnp.float32
BF16 = jnp.bfloat16
VMEM = pltpu.VMEM
NT = (((1,), (1,)), ((), ()))


def split3(value):
    high = value.astype(BF16).astype(F32)
    rest = value - high
    middle = rest.astype(BF16).astype(F32)
    return high, middle, (rest - middle).astype(BF16).astype(F32)


def queries_kernel(nope, queries_ref, latent_ref, gain_ref, sent_hbm, tile_ref, sems):
    by_head = jnp.swapaxes(queries_ref[...].astype(F32), 0, 1)
    rows = by_head.reshape(64, by_head.shape[2])
    rotated = jnp.concatenate([rows[:32, nope:], rows[32:, nope:]], 1)
    gain = jnp.concatenate([gain_ref[...].astype(F32), jnp.zeros((7, 32), F32)], 0)
    extra = jnp.concatenate([latent_ref[...].astype(F32), gain, jnp.zeros((8, 64), F32)], 1)
    extra = jnp.concatenate([extra, jnp.zeros((8, 128), F32)], 0)
    tile_ref[...] = jnp.concatenate([rows[:, :nope], rotated, extra], 0).astype(BF16)
    copies = [
        pltpu.make_async_copy(tile_ref, sent_hbm.at[chip], sems.at[chip]) for chip in range(CHIPS)
    ]
    for copy in copies:
        copy.start()
    for copy in copies:
        copy.wait()


def own_kernel(q_ref, wuk_ref, full_ref):
    q = q_ref[0]
    parts = []
    for pair in range(4):
        two = q[16 * pair : 16 * pair + 16]
        first = jnp.dot(two, wuk_ref[2 * pair], preferred_element_type=F32)
        second = jnp.dot(two, wuk_ref[2 * pair + 1], preferred_element_type=F32)
        parts += [first[:8], second[8:]]
    absorbed = jnp.concatenate(parts, 0)
    rotated = q[64:96].astype(F32)
    rotated = jnp.concatenate([rotated[:, :64], rotated[:, 64:]], 0)
    full_ref[...] = jnp.concatenate([absorbed, rotated], -1).astype(BF16)


def main_kernel(
    width,
    q_ref,
    ka_hbm,
    kb_hbm,
    wuk_ref,
    wuv_hbm,
    out_ref,
    stats_ref,
    ka_ref,
    kb_ref,
    wuv_ref,
    sems,
):
    scale = float(width) ** (-0.5)
    copies = [
        pltpu.make_async_copy(source, target, sems.at[i])
        for i, (source, target) in enumerate(
            [
                (ka_hbm, ka_ref),
                (kb_hbm, kb_ref),
                (wuv_hbm, wuv_ref),
            ]
        )
    ]
    copies[0].start()
    latent = wuk_ref.shape[2]

    def absorb(pair):
        both = q_ref[:, 16 * pair : 16 * pair + 16, :].astype(F32).reshape(CHIPS, 2, 8, -1)
        top, side = 64 + 16 * (pair % 2), 64 * (pair // 2)
        rotated = q_ref[:, top : top + 16, :].astype(F32)[:, :, side : side + 64]
        rotated = rotated.reshape(CHIPS, 2, 8, -1)
        fulls = []
        for j in range(2):
            one = both[:, j].reshape(128, -1).astype(BF16)
            absorbed = jnp.dot(one, wuk_ref[2 * pair + j], preferred_element_type=F32)
            last = rotated[:, j].reshape(128, -1)
            fulls.append(jnp.concatenate([absorbed, last], -1).astype(BF16))
        return fulls

    fulls = []
    for pair in range(4):
        fulls += absorb(pair)
    copies[0].wait()
    copies[1].start()
    copies[2].start()
    full = jnp.concatenate(fulls, 0)

    half = ka_ref.shape[1] // 2
    blocks = [(keys, i * half) for keys in (ka_ref, kb_ref) for i in range(2)]

    def score(keys, at):
        return jnp.dot(full, keys[:, at : at + half], preferred_element_type=F32)

    scores = score(*blocks[0])
    peak = None
    for i, (keys, at) in enumerate(blocks):
        if i == 1:
            copies[1].wait()
            copies[2].wait()
        later = score(*blocks[i + 1]) if i < 3 else None
        top = jnp.max(scores, -1, keepdims=True)
        top = top if peak is None else jnp.maximum(peak, top)
        expd = jnp.exp2((scores - top) * (scale * LOG2E))
        part = lax.dot_general(
            expd.astype(BF16), keys[:latent, at : at + half], NT, preferred_element_type=F32
        )
        if peak is None:
            mass, acc = jnp.sum(expd, -1, keepdims=True), part
        else:
            fade = jnp.exp2((peak - top) * (scale * LOG2E))
            mass = mass * fade + jnp.sum(expd, -1, keepdims=True)
            acc = acc * fade + part
        peak, scores = top, later

    attn = (acc / mass).astype(BF16)
    lane = lax.broadcasted_iota(jnp.int32, (128, 128), 1)
    stats = jnp.zeros((128, 128), F32)
    for pair in range(4):
        values = []
        for j in range(2):
            head = 2 * pair + j
            here = slice(128 * head, 128 * head + 128)
            values.append(
                jnp.dot(attn[here], wuv_ref[head], preferred_element_type=F32).reshape(
                    CHIPS, 8, 128
                )
            )
            for k, piece in enumerate(split3(peak[here]) + split3(mass[here])):
                stats = jnp.where(lane == 8 * k + head, piece, stats)
        out_ref[:, 16 * pair : 16 * pair + 16, :] = jnp.concatenate(values, 1).astype(BF16)
    stats_ref[...] = stats.reshape(CHIPS, 8, 128)


def attach_kernel(values_ref, stats_ref, moved_ref, out_ref):
    moved = moved_ref[...].astype(F32)[:, :8, :]
    out_ref[:, :64, :] = values_ref[...]
    out_ref[:, 64:80, :] = jnp.concatenate([stats_ref[...], moved], 1).astype(BF16)


def attend(scale, full, blocks, wuv_ref):
    latent = wuv_ref.shape[1]
    scores = []
    for live, keys in blocks:
        raw = jnp.dot(full, keys, preferred_element_type=F32)
        scores.append(jnp.where(live, raw, -jnp.inf))
    peak = functools.reduce(jnp.maximum, [jnp.max(s, -1, keepdims=True) for s in scores])
    mass, acc = 0.0, 0.0
    for s, (_, keys) in zip(scores, blocks):
        p = jnp.exp2((s - peak) * (scale * LOG2E))
        mass = mass + jnp.sum(p, -1, keepdims=True)
        acc = acc + lax.dot_general(
            p.astype(BF16), keys[:latent], NT, preferred_element_type=F32
        )
    attn = (acc / mass).astype(BF16)
    lane = lax.broadcasted_iota(jnp.int32, (8, 128), 1)
    peaks = masses = jnp.zeros((8, 128), F32)
    values = []
    for pair in range(4):
        two = attn[16 * pair : 16 * pair + 16]
        first = jnp.dot(two, wuv_ref[2 * pair], preferred_element_type=F32)
        second = jnp.dot(two, wuv_ref[2 * pair + 1], preferred_element_type=F32)
        values += [first[:8], second[8:]]
    for head in range(8):
        here = slice(8 * head, 8 * head + 8)
        peaks = jnp.where(lane == head, peak[here], peaks)
        masses = jnp.where(lane == head, mass[here], masses)
    return values, peaks, masses


def suffix_kernel(scale, full_ref, suffix_ref, lengths_ref, wuv_ref, out_ref, stats_ref):
    gen = suffix_ref.shape[2]
    row = lax.broadcasted_iota(jnp.int32, (64, gen), 0) % 8
    col = lax.broadcasted_iota(jnp.int32, (64, gen), 1)
    blocks = [
        ((row // 4 == sample) & (col < lengths_ref[sample]), suffix_ref[sample])
        for sample in range(2)
    ]
    values, peaks, masses = attend(scale, full_ref[...], blocks, wuv_ref)
    out_ref[...] = jnp.concatenate(values, 0)
    stats_ref[...] = jnp.concatenate([peaks, masses], 0)


def combine_kernel(
    scale, got_ref, suffix_ref, suffix_stats_ref, full_ref, rope_ref, wuv_ref, out_ref
):
    place = lax.axis_index("z")
    lane = lax.broadcasted_iota(jnp.int32, (8, 128), 1) // 32
    latents, gains = [], []
    for g in range(4):
        latent, gain = 0.0, 0.0
        for j in range(4):
            chip = ((place - (4 * g + j)) & 15) ^ 8
            piece = got_ref[chip, 64:80, :].astype(F32)[8:]
            one = jnp.where(lane == 0, piece, 0.0)
            latent = latent + (pltpu.roll(one, 32 * j, 1) if j else one)
            one = jnp.where(lane == 1, piece, 0.0)
            shift = (32 * (j - 1)) % 128
            gain = gain + (pltpu.roll(one, shift, 1) if shift else one)
        latents.append(latent)
        gains.append(gain)
    plain, gain = jnp.concatenate(latents, -1), jnp.concatenate(gains, -1)[:1]
    square = jnp.sum(plain * plain, -1, keepdims=True) / plain.shape[1]
    normed = plain * lax.rsqrt(square + eps) * gain
    fresh = jnp.concatenate([normed, rope_ref[...].astype(F32)], -1)
    fresh = jnp.concatenate([fresh, jnp.zeros((120, fresh.shape[1]), F32)], 0)
    row = lax.broadcasted_iota(jnp.int32, (64, 128), 0) % 8
    col = lax.broadcasted_iota(jnp.int32, (64, 128), 1)
    live = (col < 8) & (col // 4 == row // 4) & (col <= row)
    fresh_values, fresh_peak, fresh_mass = attend(
        scale, full_ref[...], [(live, fresh.T.astype(BF16))], wuv_ref
    )

    raw = got_ref[:, 64:80, :].astype(F32)[:, :8, :].reshape(128, 128)

    def lanes(k):
        return raw if k == 0 else pltpu.roll(raw, 128 - 8 * k, 1)

    peaks = (lanes(0) + lanes(1) + lanes(2)).reshape(CHIPS, 8, 128)
    masses = (lanes(3) + lanes(4) + lanes(5)).reshape(CHIPS, 8, 128)
    suffix_peak, suffix_mass = suffix_stats_ref[:8], suffix_stats_ref[8:]
    peak = jnp.maximum(jnp.max(peaks, 0), jnp.maximum(suffix_peak, fresh_peak))
    weights = jnp.exp2((peaks - peak[None]) * (scale * LOG2E)) * masses
    suffix_weight = jnp.exp2((suffix_peak - peak) * (scale * LOG2E)) * suffix_mass
    fresh_weight = jnp.exp2((fresh_peak - peak) * (scale * LOG2E)) * fresh_mass
    inverse = 1.0 / (jnp.sum(weights, 0) + suffix_weight + fresh_weight)
    for pair in range(4):
        got = got_ref[:, 16 * pair : 16 * pair + 16, :].astype(F32)
        for j in range(2):
            head = 2 * pair + j
            this = slice(head, head + 1)
            total = suffix_weight[:, this] * suffix_ref[8 * head : 8 * head + 8, :]
            total = total + fresh_weight[:, this] * fresh_values[head]
            for chip in range(CHIPS):
                total = total + weights[chip, :, this] * got[chip, 8 * j : 8 * j + 8, :]
            total = total * inverse[:, this]
            out_ref[:, 128 * head : 128 * head + 128] = total.astype(BF16)


def call(kernel, outs, n_in, smem=(), hbm=(), scratch=(), cost=1, mib=24):
    spaces = [pltpu.SMEM if i in smem else pl.ANY if i in hbm else VMEM for i in range(n_in)]
    return pl.pallas_call(
        kernel,
        out_shape=outs,
        in_specs=[pl.BlockSpec(memory_space=space) for space in spaces],
        out_specs=jax.tree.map(lambda _: pl.BlockSpec(memory_space=VMEM), outs),
        scratch_shapes=scratch,
        compiler_params=pltpu.CompilerParams(vmem_limit_bytes=mib * 1024 * 1024),
        cost_estimate=pl.CostEstimate(
            flops=cost * 10**9, transcendentals=0, bytes_accessed=0
        ),
    )


def per_device(
    queries, prompt_cache, suffix_cache, gen_lengths, new_latent, new_rope, latent_gain, w_uk, w_uv
):
    width = queries.shape[2]
    scale = float(width) ** (-0.5)
    sent = pl.pallas_call(
        functools.partial(queries_kernel, w_uk.shape[1]),
        out_shape=jax.ShapeDtypeStruct((CHIPS, 112, 128), BF16),
        in_specs=[pl.BlockSpec(memory_space=VMEM)] * 3,
        out_specs=pl.BlockSpec(memory_space=pl.ANY),
        scratch_shapes=[VMEM((112, 128), BF16), pltpu.SemaphoreType.DMA((CHIPS,))],
        compiler_params=pltpu.CompilerParams(vmem_limit_bytes=62 * 1024 * 1024),
    )(queries, new_latent, latent_gain[None])
    gathered = lax.all_to_all(sent, PLANE, 0, 0, axis_index_groups=[ORDER], tiled=True)
    keys = prompt_cache.T
    other = lax.ppermute(keys, "core", [(0, 1), (1, 0)])
    full = call(
        own_kernel,
        jax.ShapeDtypeStruct((64, keys.shape[0]), BF16),
        2,
        cost=30,
    )(sent, w_uk)

    moves = [
        ((2 * p + core) * 16 + z, (2 * p + core) * 16 + (z + (8 ^ k)) % 16)
        for k, p in enumerate(ORDER)
        for core in range(2)
        for z in range(16)
    ]
    moved = lax.ppermute(gathered[:, 96:, :], ("y", "x", "core", "z"), moves)

    values, stats = call(
        functools.partial(main_kernel, width),
        (
            jax.ShapeDtypeStruct((CHIPS, 64, 128), BF16),
            jax.ShapeDtypeStruct((CHIPS, 8, 128), F32),
        ),
        5,
        hbm=(1, 2, 4),
        scratch=[
            VMEM(keys.shape, BF16),
            VMEM(keys.shape, BF16),
            VMEM(w_uv.shape, BF16),
            pltpu.SemaphoreType.DMA((3,)),
        ],
        cost=8,
        mib=52,
    )(gathered, keys, other, w_uk, w_uv)
    parts = call(attach_kernel, jax.ShapeDtypeStruct((CHIPS, 80, 128), BF16), 3)(
        values, stats, moved
    )
    got = lax.all_to_all(parts, PLANE, 0, 0, axis_index_groups=[ORDER], tiled=True)
    suffix, suffix_stats = call(
        functools.partial(suffix_kernel, scale),
        (jax.ShapeDtypeStruct((64, 128), F32), jax.ShapeDtypeStruct((16, 128), F32)),
        4,
        smem=(2,),
        cost=5,
    )(full, jnp.swapaxes(suffix_cache, 1, 2), gen_lengths, w_uv)
    return call(
        functools.partial(combine_kernel, scale), jax.ShapeDtypeStruct((8, 1024), BF16), 6
    )(got, suffix, suffix_stats, full, new_rope, w_uv)


def solution(mesh):
    fine = Mesh(mesh.devices.reshape(4, 4, 2, 16), ("y", "x", "core", "z"))
    seq = ("y", "x", "core")
    return jax.shard_map(
        per_device,
        mesh=fine,
        in_specs=(
            P(seq, "z", None),
            P(seq, None),
            P(seq, None, None),
            P(seq),
            P(seq, "z"),
            P(seq, None),
            P("z"),
            P("z", None, None),
            P("z", None, None),
        ),
        out_specs=P(seq, "z"),
        check_vma=False,
    )
```

```python
import functools

import jax
import jax.numpy as jnp
from jax import lax
from jax.experimental import pallas as pl
from jax.experimental.pallas import tpu as pltpu
from jax.sharding import Mesh
from jax.sharding import PartitionSpec as P

eps = 1e-06
LOG2E = 1.4426950408889634
CHIPS = 16
PLANE = ("y", "x")
ORDER = sorted(
    range(CHIPS), key=lambda p: (abs(p // 4 - 2) + min((p - 2) % 4, (2 - p) % 4), p)
)
F32 = jnp.float32
BF16 = jnp.bfloat16
VMEM = pltpu.VMEM
NT = (((1,), (1,)), ((), ()))


def split3(value):
    high = value.astype(BF16).astype(F32)
    rest = value - high
    middle = rest.astype(BF16).astype(F32)
    return high, middle, (rest - middle).astype(BF16).astype(F32)


def queries_kernel(nope, queries_ref, latent_ref, gain_ref, sent_hbm, tile_ref, sems):
    by_head = jnp.swapaxes(queries_ref[...].astype(F32), 0, 1)
    rows = by_head.reshape(64, by_head.shape[2])
    rotated = jnp.concatenate([rows[:32, nope:], rows[32:, nope:]], 1)
    gain = jnp.concatenate([gain_ref[...].astype(F32), jnp.zeros((7, 32), F32)], 0)
    extra = jnp.concatenate([latent_ref[...].astype(F32), gain, jnp.zeros((8, 64), F32)], 1)
    extra = jnp.concatenate([extra, jnp.zeros((8, 128), F32)], 0)
    tile_ref[...] = jnp.concatenate([rows[:, :nope], rotated, extra], 0).astype(BF16)
    copies = [
        pltpu.make_async_copy(tile_ref, sent_hbm.at[chip], sems.at[chip]) for chip in range(CHIPS)
    ]
    for copy in copies:
        copy.start()
    for copy in copies:
        copy.wait()


def own_kernel(q_ref, wuk_ref, full_ref):
    q = q_ref[0]
    parts = []
    for pair in range(4):
        two = q[16 * pair : 16 * pair + 16]
        first = jnp.dot(two, wuk_ref[2 * pair], preferred_element_type=F32)
        second = jnp.dot(two, wuk_ref[2 * pair + 1], preferred_element_type=F32)
        parts += [first[:8], second[8:]]
    absorbed = jnp.concatenate(parts, 0)
    rotated = q[64:96].astype(F32)
    rotated = jnp.concatenate([rotated[:, :64], rotated[:, 64:]], 0)
    full_ref[...] = jnp.concatenate([absorbed, rotated], -1).astype(BF16)


def main_kernel(
    width,
    q_ref,
    ka_hbm,
    kb_hbm,
    wuk_ref,
    wuv_hbm,
    out_ref,
    stats_ref,
    ka_ref,
    kb_ref,
    wuv_ref,
    sems,
):
    scale = float(width) ** (-0.5)
    copies = [
        pltpu.make_async_copy(source, target, sems.at[i])
        for i, (source, target) in enumerate(
            [
                (ka_hbm, ka_ref),
                (kb_hbm, kb_ref),
                (wuv_hbm, wuv_ref),
            ]
        )
    ]
    copies[0].start()
    latent = wuk_ref.shape[2]

    def absorb(pair):
        both = q_ref[:, 16 * pair : 16 * pair + 16, :].astype(F32).reshape(CHIPS, 2, 8, -1)
        top, side = 64 + 16 * (pair % 2), 64 * (pair // 2)
        rotated = q_ref[:, top : top + 16, :].astype(F32)[:, :, side : side + 64]
        rotated = rotated.reshape(CHIPS, 2, 8, -1)
        fulls = []
        for j in range(2):
            one = both[:, j].reshape(128, -1).astype(BF16)
            absorbed = jnp.dot(one, wuk_ref[2 * pair + j], preferred_element_type=F32)
            last = rotated[:, j].reshape(128, -1)
            fulls.append(jnp.concatenate([absorbed, last], -1).astype(BF16))
        return fulls

    fulls = []
    for pair in range(4):
        fulls += absorb(pair)
    copies[0].wait()
    copies[1].start()
    copies[2].start()
    full = jnp.concatenate(fulls, 0)

    half = ka_ref.shape[1] // 2
    blocks = [(keys, i * half) for keys in (ka_ref, kb_ref) for i in range(2)]

    def score(keys, at):
        return jnp.dot(full, keys[:, at : at + half], preferred_element_type=F32)

    scores = score(*blocks[0])
    peak = None
    for i, (keys, at) in enumerate(blocks):
        if i == 1:
            copies[1].wait()
            copies[2].wait()
        later = score(*blocks[i + 1]) if i < 3 else None
        top = jnp.max(scores, -1, keepdims=True)
        top = top if peak is None else jnp.maximum(peak, top)
        expd = jnp.exp2((scores - top) * (scale * LOG2E))
        part = lax.dot_general(
            expd.astype(BF16), keys[:latent, at : at + half], NT, preferred_element_type=F32
        )
        if peak is None:
            mass, acc = jnp.sum(expd, -1, keepdims=True), part
        else:
            fade = jnp.exp2((peak - top) * (scale * LOG2E))
            mass = mass * fade + jnp.sum(expd, -1, keepdims=True)
            acc = acc * fade + part
        peak, scores = top, later

    attn = (acc / mass).astype(BF16)
    lane = lax.broadcasted_iota(jnp.int32, (128, 128), 1)
    stats = jnp.zeros((128, 128), F32)
    for pair in range(4):
        values = []
        for j in range(2):
            head = 2 * pair + j
            here = slice(128 * head, 128 * head + 128)
            values.append(
                jnp.dot(attn[here], wuv_ref[head], preferred_element_type=F32).reshape(
                    CHIPS, 8, 128
                )
            )
            for k, piece in enumerate(split3(peak[here]) + split3(mass[here])):
                stats = jnp.where(lane == 8 * k + head, piece, stats)
        out_ref[:, 16 * pair : 16 * pair + 16, :] = jnp.concatenate(values, 1).astype(BF16)
    stats_ref[...] = stats.reshape(CHIPS, 8, 128)


def attach_kernel(values_ref, stats_ref, moved_ref, out_ref):
    moved = moved_ref[...].astype(F32)[:, :8, :]
    out_ref[:, :64, :] = values_ref[...]
    out_ref[:, 64:80, :] = jnp.concatenate([stats_ref[...], moved], 1).astype(BF16)


def attend(scale, full, blocks, wuv_ref):
    latent = wuv_ref.shape[1]
    scores = []
    for live, keys in blocks:
        raw = jnp.dot(full, keys, preferred_element_type=F32)
        scores.append(jnp.where(live, raw, -jnp.inf))
    peak = functools.reduce(jnp.maximum, [jnp.max(s, -1, keepdims=True) for s in scores])
    mass, acc = 0.0, 0.0
    for s, (_, keys) in zip(scores, blocks):
        p = jnp.exp2((s - peak) * (scale * LOG2E))
        mass = mass + jnp.sum(p, -1, keepdims=True)
        acc = acc + lax.dot_general(
            p.astype(BF16), keys[:latent], NT, preferred_element_type=F32
        )
    attn = (acc / mass).astype(BF16)
    lane = lax.broadcasted_iota(jnp.int32, (8, 128), 1)
    peaks = masses = jnp.zeros((8, 128), F32)
    values = []
    for pair in range(4):
        two = attn[16 * pair : 16 * pair + 16]
        first = jnp.dot(two, wuv_ref[2 * pair], preferred_element_type=F32)
        second = jnp.dot(two, wuv_ref[2 * pair + 1], preferred_element_type=F32)
        values += [first[:8], second[8:]]
    for head in range(8):
        here = slice(8 * head, 8 * head + 8)
        peaks = jnp.where(lane == head, peak[here], peaks)
        masses = jnp.where(lane == head, mass[here], masses)
    return values, peaks, masses


def suffix_kernel(scale, full_ref, suffix_ref, lengths_ref, wuv_ref, out_ref, stats_ref):
    gen = suffix_ref.shape[2]
    row = lax.broadcasted_iota(jnp.int32, (64, gen), 0) % 8
    col = lax.broadcasted_iota(jnp.int32, (64, gen), 1)
    blocks = [
        ((row // 4 == sample) & (col < lengths_ref[sample]), suffix_ref[sample])
        for sample in range(2)
    ]
    values, peaks, masses = attend(scale, full_ref[...], blocks, wuv_ref)
    out_ref[...] = jnp.concatenate(values, 0)
    stats_ref[...] = jnp.concatenate([peaks, masses], 0)


def combine_kernel(
    scale, got_ref, suffix_ref, suffix_stats_ref, full_ref, rope_ref, wuv_ref, out_ref
):
    place = lax.axis_index("z")
    lane = lax.broadcasted_iota(jnp.int32, (8, 128), 1) // 32
    latents, gains = [], []
    for g in range(4):
        latent, gain = 0.0, 0.0
        for j in range(4):
            away = ((place - (4 * g + j)) & 15) - 8
            chip = jnp.minimum(jnp.where(away > 0, 2 * away - 1, -2 * away), 15)
            piece = got_ref[chip, 64:80, :].astype(F32)[8:]
            one = jnp.where(lane == 0, piece, 0.0)
            latent = latent + (pltpu.roll(one, 32 * j, 1) if j else one)
            one = jnp.where(lane == 1, piece, 0.0)
            shift = (32 * (j - 1)) % 128
            gain = gain + (pltpu.roll(one, shift, 1) if shift else one)
        latents.append(latent)
        gains.append(gain)
    plain, gain = jnp.concatenate(latents, -1), jnp.concatenate(gains, -1)[:1]
    square = jnp.sum(plain * plain, -1, keepdims=True) / plain.shape[1]
    normed = plain * lax.rsqrt(square + eps) * gain
    fresh = jnp.concatenate([normed, rope_ref[...].astype(F32)], -1)
    fresh = jnp.concatenate([fresh, jnp.zeros((120, fresh.shape[1]), F32)], 0)
    row = lax.broadcasted_iota(jnp.int32, (64, 128), 0) % 8
    col = lax.broadcasted_iota(jnp.int32, (64, 128), 1)
    live = (col < 8) & (col // 4 == row // 4) & (col <= row)
    fresh_values, fresh_peak, fresh_mass = attend(
        scale, full_ref[...], [(live, fresh.T.astype(BF16))], wuv_ref
    )

    raw = got_ref[:, 64:80, :].astype(F32)[:, :8, :].reshape(128, 128)

    def lanes(k):
        return raw if k == 0 else pltpu.roll(raw, 128 - 8 * k, 1)

    peaks = (lanes(0) + lanes(1) + lanes(2)).reshape(CHIPS, 8, 128)
    masses = (lanes(3) + lanes(4) + lanes(5)).reshape(CHIPS, 8, 128)
    suffix_peak, suffix_mass = suffix_stats_ref[:8], suffix_stats_ref[8:]
    peak = jnp.maximum(jnp.max(peaks, 0), jnp.maximum(suffix_peak, fresh_peak))
    weights = jnp.exp2((peaks - peak[None]) * (scale * LOG2E)) * masses
    suffix_weight = jnp.exp2((suffix_peak - peak) * (scale * LOG2E)) * suffix_mass
    fresh_weight = jnp.exp2((fresh_peak - peak) * (scale * LOG2E)) * fresh_mass
    inverse = 1.0 / (jnp.sum(weights, 0) + suffix_weight + fresh_weight)
    for pair in range(4):
        got = got_ref[:, 16 * pair : 16 * pair + 16, :].astype(F32)
        for j in range(2):
            head = 2 * pair + j
            this = slice(head, head + 1)
            total = suffix_weight[:, this] * suffix_ref[8 * head : 8 * head + 8, :]
            total = total + fresh_weight[:, this] * fresh_values[head]
            for chip in range(CHIPS):
                total = total + weights[chip, :, this] * got[chip, 8 * j : 8 * j + 8, :]
            total = total * inverse[:, this]
            out_ref[:, 128 * head : 128 * head + 128] = total.astype(BF16)


def call(kernel, outs, n_in, smem=(), hbm=(), scratch=(), cost=1, mib=24):
    spaces = [pltpu.SMEM if i in smem else pl.ANY if i in hbm else VMEM for i in range(n_in)]
    return pl.pallas_call(
        kernel,
        out_shape=outs,
        in_specs=[pl.BlockSpec(memory_space=space) for space in spaces],
        out_specs=jax.tree.map(lambda _: pl.BlockSpec(memory_space=VMEM), outs),
        scratch_shapes=scratch,
        compiler_params=pltpu.CompilerParams(vmem_limit_bytes=mib * 1024 * 1024),
        cost_estimate=pl.CostEstimate(
            flops=cost * 10**9, transcendentals=0, bytes_accessed=0
        ),
    )


def per_device(
    queries, prompt_cache, suffix_cache, gen_lengths, new_latent, new_rope, latent_gain, w_uk, w_uv
):
    width = queries.shape[2]
    scale = float(width) ** (-0.5)
    sent = pl.pallas_call(
        functools.partial(queries_kernel, w_uk.shape[1]),
        out_shape=jax.ShapeDtypeStruct((CHIPS, 112, 128), BF16),
        in_specs=[pl.BlockSpec(memory_space=VMEM)] * 3,
        out_specs=pl.BlockSpec(memory_space=pl.ANY),
        scratch_shapes=[VMEM((112, 128), BF16), pltpu.SemaphoreType.DMA((CHIPS,))],
        compiler_params=pltpu.CompilerParams(vmem_limit_bytes=62 * 1024 * 1024),
    )(queries, new_latent, latent_gain[None])
    gathered = lax.all_to_all(sent, PLANE, 0, 0, axis_index_groups=[ORDER], tiled=True)
    keys = prompt_cache.T
    other = lax.ppermute(keys, "core", [(0, 1), (1, 0)])
    full = call(
        own_kernel,
        jax.ShapeDtypeStruct((64, keys.shape[0]), BF16),
        2,
        cost=30,
    )(sent, w_uk)

    def step(k):
        return 8 + (k // 2 + 1 if k % 2 else -(k // 2))

    moves = [
        ((2 * p + core) * 16 + z, (2 * p + core) * 16 + (z + step(k)) % 16)
        for k, p in enumerate(ORDER)
        for core in range(2)
        for z in range(16)
    ]
    moved = lax.ppermute(gathered[:, 96:, :], ("y", "x", "core", "z"), moves)

    values, stats = call(
        functools.partial(main_kernel, width),
        (
            jax.ShapeDtypeStruct((CHIPS, 64, 128), BF16),
            jax.ShapeDtypeStruct((CHIPS, 8, 128), F32),
        ),
        5,
        hbm=(1, 2, 4),
        scratch=[
            VMEM(keys.shape, BF16),
            VMEM(keys.shape, BF16),
            VMEM(w_uv.shape, BF16),
            pltpu.SemaphoreType.DMA((3,)),
        ],
        cost=8,
        mib=52,
    )(gathered, keys, other, w_uk, w_uv)
    parts = call(attach_kernel, jax.ShapeDtypeStruct((CHIPS, 80, 128), BF16), 3)(
        values, stats, moved
    )
    got = lax.all_to_all(parts, PLANE, 0, 0, axis_index_groups=[ORDER], tiled=True)
    suffix, suffix_stats = call(
        functools.partial(suffix_kernel, scale),
        (jax.ShapeDtypeStruct((64, 128), F32), jax.ShapeDtypeStruct((16, 128), F32)),
        4,
        smem=(2,),
        cost=5,
    )(full, jnp.swapaxes(suffix_cache, 1, 2), gen_lengths, w_uv)
    return call(
        functools.partial(combine_kernel, scale), jax.ShapeDtypeStruct((8, 1024), BF16), 6
    )(got, suffix, suffix_stats, full, new_rope, w_uv)


def solution(mesh):
    fine = Mesh(mesh.devices.reshape(4, 4, 2, 16), ("y", "x", "core", "z"))
    seq = ("y", "x", "core")
    return jax.shard_map(
        per_device,
        mesh=fine,
        in_specs=(
            P(seq, "z", None),
            P(seq, None),
            P(seq, None, None),
            P(seq),
            P(seq, "z"),
            P(seq, None),
            P("z"),
            P("z", None, None),
            P("z", None, None),
        ),
        out_specs=P(seq, "z"),
        check_vma=False,
    )
```
